512 devices in a mesh: depth: 64 (over y_lo, z, core), grp: 8 (over y_hi, x).
Axes of the slice: x: 4, y: 4 (y_hi: 2, y_lo: 2; y = y_hi * 2 + y_lo), z: 16, core: 2. Of those that a mesh axis runs over, the one named last changes fastest.
Arguments:
- inputs: bfloat16 [16, 128, 128, 256], P(None, 'depth', 'grp'), may hold values from -6 to 6
- weight_two: bfloat16 [3, 3, 3, 32, 16], replicated, may hold values from -0.3125 to 0.3125
- weight_three: bfloat16 [3, 3, 3, 64, 32], P(None, None, None, 'grp'), may hold values from -0.21875 to 0.21875
- cotangent: bfloat16 [64, 64, 64, 128], P('grp', 'depth'), may hold values from -6 to 6
Outputs:
- input_grad: bfloat16 [16, 128, 128, 256], P(None, 'depth', 'grp')
- weight_grad_two: float32 [3, 3, 3, 32, 16], replicated
- weight_grad_three: float32 [3, 3, 3, 64, 32], P(None, None, None, 'grp')
The draws below stay inside these ranges and needn't reach their ends.
All inputs are finite; a program needn't handle non-finite values.
Results may differ from the reference program's by a relative error of at most 0.02.
Values may be sent and summed in bfloat16 or wider, within the bound.
No kernel may reach another device: no remote copies, remote signals or barrier semaphores. Data moves between devices by JAX's collectives and lax.ppermute only.
A program may use at most 128 MiB of HBM per device.

```python
import math
import jax
import jax.numpy as jnp
from jax import lax

CIN = 16
F2 = 32
F3 = 64
WIDTH = 256
DEPTH = 128
HEIGHT = 128


def steps_of(key, extent, shards, smallest, high):
    factor_of = 1.0
    for axis_at, blocks in shards:
        draws = jax.random.uniform(jax.random.fold_in(jax.random.fold_in(key, 6), axis_at), (blocks,), jnp.float32, smallest / len(shards), high / len(shards))
        factor_of = factor_of * jnp.repeat(jnp.exp(draws), extent[axis_at] // blocks).reshape((-1,) + (1,) * (len(extent) - 1 - axis_at))
    return factor_of


def normal_values(own_key, dims, scale, limit, cuts=(), kind=jnp.bfloat16):
    result = jax.random.normal(own_key, dims, jnp.float32) * scale
    if len(cuts) > 0:
        result = steps_of(own_key, dims, cuts, -0.22, 0.18) * result
    return jnp.clip(result, min=-limit, max=limit).astype(kind)


def setup_inputs(seed: int = 0) -> dict:
    key_list = jax.random.split(jax.random.key(seed), 5)
    return {
        "inputs": normal_values(key_list[0], (CIN, DEPTH, HEIGHT, WIDTH), 1.0, 6.0, ((1, 64), (2, 8))),
        "weight_two": normal_values(key_list[1], (3, 3, 3, F2, CIN), (27 * CIN) ** -0.5, 0.3125),
        "weight_three": normal_values(key_list[2], (3, 3, 3, F3, F2), (27 * F2) ** -0.5, 0.21875, ((3, 8),)),
        "cotangent": normal_values(key_list[3], (F3, DEPTH // 2, HEIGHT // 2, WIDTH // 2), 1.0, 6.0, ((0, 8), (1, 64))),
    }


def activate(values):
    return 0.3 * values + 0.7 * jax.nn.softplus(values)

def derivative(values):
    return 0.3 + 0.7 * jax.nn.sigmoid(values)

def convolve(padded, weights):
    planes = padded.shape[1] - 2
    height = padded.shape[2] - 2
    breadth = padded.shape[3] - 2
    summed = jnp.zeros((weights.shape[3], planes, height, breadth), jnp.float32)
    data = padded.astype(jnp.float32)
    for depth_off in range(3):
        for row_off in range(3):
            for col_off in range(3):
                window = data[:, depth_off:depth_off + planes, row_off:row_off + height, col_off:col_off + breadth]
                summed = summed + jnp.einsum('fc,cdhw->fdhw', weights[depth_off, row_off, col_off].astype(jnp.float32), window)
    return summed

def convolve_back(padded, weights):
    planes = padded.shape[1] - 2
    height = padded.shape[2] - 2
    breadth = padded.shape[3] - 2
    summed = jnp.zeros((weights.shape[4], planes, height, breadth), jnp.float32)
    data = padded.astype(jnp.float32)
    for depth_off in range(3):
        for row_off in range(3):
            for col_off in range(3):
                window = data[:, 2 - depth_off:2 - depth_off + planes, 2 - row_off:2 - row_off + height, 2 - col_off:2 - col_off + breadth]
                summed = summed + jnp.einsum('fc,fdhw->cdhw', weights[depth_off, row_off, col_off].astype(jnp.float32), window)
    return summed

def filter_grad(grads, padded):
    planes, height, breadth = (grads.shape[1], grads.shape[2], grads.shape[3])
    data = padded.astype(jnp.float32)
    left = grads.astype(jnp.float32)
    pieces = []
    for depth_off in range(3):
        for row_off in range(3):
            for col_off in range(3):
                window = data[:, depth_off:depth_off + planes, row_off:row_off + height, col_off:col_off + breadth]
                pieces.append(jnp.einsum('fdhw,cdhw->fc', left, window))
    stacked = jnp.stack(pieces)
    return stacked.reshape(3, 3, 3, stacked.shape[1], stacked.shape[2])

def reference(inputs, weight_two, weight_three, cotangent):
    chans, planes, height, breadth = inputs.shape
    filters = weight_two.shape[3]
    half = planes // 2
    padded_in = jnp.pad(inputs, ((0, 0), (1, 1), (1, 1), (1, 1)))
    indices = jnp.arange(half, dtype=jnp.int32)

    def forward_plane(index):
        slab = lax.dynamic_slice_in_dim(padded_in, (2 * index).astype(jnp.int32), 4, 1)
        pre_two = convolve(slab, weight_two)
        shaped = activate(pre_two).reshape(filters, 1, 2, height // 2, 2, breadth // 2, 2)
        return shaped.mean(axis=(2, 4, 6)).astype(jnp.bfloat16)[:, 0]
    pooled = jnp.moveaxis(lax.map(forward_plane, indices), 0, 1)
    padded_pool = jnp.pad(pooled, ((0, 0), (1, 1), (1, 1), (1, 1)))

    def third_plane(index):
        slab = lax.dynamic_slice_in_dim(padded_pool, index.astype(jnp.int32), 3, 1)
        pre_three = convolve(slab, weight_three)
        upstream = lax.dynamic_slice_in_dim(cotangent, index.astype(jnp.int32), 1, 1)
        grad_three = (upstream.astype(jnp.float32) * derivative(pre_three)).astype(jnp.bfloat16)
        return (grad_three[:, 0], filter_grad(grad_three, slab))
    grads_three, parts_three = lax.map(third_plane, indices)
    grad_three = jnp.moveaxis(grads_three, 0, 1)
    weight_grad_three = lax.optimization_barrier(jnp.sum(parts_three, axis=0)) / math.sqrt(planes * height * breadth / 8)
    padded_three = jnp.pad(grad_three, ((0, 0), (1, 1), (1, 1), (1, 1)))

    def second_plane(index):
        slab = lax.dynamic_slice_in_dim(padded_three, index.astype(jnp.int32), 3, 1)
        pooled_grad = convolve_back(slab, weight_three)
        xslab = lax.dynamic_slice_in_dim(padded_in, (2 * index).astype(jnp.int32), 4, 1)
        pre_two = convolve(xslab, weight_two)
        spread = jnp.repeat(jnp.repeat(jnp.repeat(pooled_grad, 2, 1), 2, 2), 2, 3)
        grad_two = (spread * 0.125 * derivative(pre_two)).astype(jnp.bfloat16)
        return (grad_two, filter_grad(grad_two, xslab))
    grads_two, parts_two = lax.map(second_plane, indices)
    grad_two = jnp.moveaxis(grads_two, 0, 1).reshape(filters, planes, height, breadth)
    weight_grad_two = lax.optimization_barrier(jnp.sum(parts_two, axis=0)) / math.sqrt(planes * height * breadth)
    padded_two = jnp.pad(grad_two, ((0, 0), (1, 1), (1, 1), (1, 1)))

    def input_plane(index):
        slab = lax.dynamic_slice_in_dim(padded_two, (2 * index).astype(jnp.int32), 4, 1)
        return convolve_back(slab, weight_two).astype(jnp.bfloat16)
    input_grad = jnp.moveaxis(lax.map(input_plane, indices), 0, 1).reshape(chans, planes, height, breadth)
    return (input_grad, weight_grad_two, weight_grad_three)
```

```python
import functools
import math

import jax
import jax.numpy as jnp
import numpy as np
from jax import lax
from jax.experimental import pallas as pl
from jax.experimental.pallas import tpu as pltpu
from jax.sharding import PartitionSpec as P


F32 = jnp.float32
BF16 = jnp.bfloat16
BREADTH = 128


def call(kernel, outs, scratch, args, flops, scalars=0):
    specs = [pl.BlockSpec(memory_space=pltpu.SMEM)] * scalars
    specs += [pl.BlockSpec(memory_space=pltpu.VMEM)] * (len(args) - scalars)
    moved = sum(math.prod(a.shape) * a.dtype.itemsize for a in list(args) + list(outs))
    return pl.pallas_call(
        kernel,
        out_shape=outs,
        in_specs=specs,
        out_specs=[pl.BlockSpec(memory_space=pltpu.VMEM)] * len(outs),
        scratch_shapes=scratch,
        compiler_params=pltpu.CompilerParams(vmem_limit_bytes=32 * 1024 * 1024),
        cost_estimate=pl.CostEstimate(flops=flops, bytes_accessed=moved, transcendentals=0),
    )(*args)


def dot(left, right):
    return jnp.dot(left, right, preferred_element_type=F32)


def dot_nt(left, right):
    return lax.dot_general(left, right, (((1,), (1,)), ((), ())), preferred_element_type=F32)


def indicator(shape, test):
    row = lax.broadcasted_iota(jnp.int32, shape, 0)
    col = lax.broadcasted_iota(jnp.int32, shape, 1)
    return jnp.where(test(row, col), 1.0, 0.0).astype(BF16)


def splitter():
    def test(row, col):
        part, at = col // BREADTH, col % BREADTH
        return row == 2 * at + part - 1

    return indicator((2 * BREADTH, 4 * BREADTH), test)


def shifter():
    def test(row, col):
        part, at = col // BREADTH, col % BREADTH
        return row == at + 2 * part - 1

    return indicator((BREADTH, 2 * BREADTH), test)


def joiner():
    def test(row, col):
        return col == 2 * (row % BREADTH) + row // BREADTH

    return indicator((2 * BREADTH, 2 * BREADTH), test)


def forward_two(first_ref, count_ref, own, below, above, top, bottom, weight, pooled, slope, parts, split):
    split[...] = splitter()
    edge = top.shape[0]
    height = own.shape[0]

    def place(row, block):
        cells = dot(block, split[...]).astype(BF16)
        for part in range(4):
            parts[row, part * 64 : part * 64 + 64, :] = cells[:, part * BREADTH : (part + 1) * BREADTH]

    def middle(row, carry):
        block = jnp.concatenate([below[row], own[row, 0], own[row, 1], above[row]], axis=0)
        place(row + edge, block)
        return carry

    lax.fori_loop(0, height, middle, 0, unroll=2)

    def ends(row, carry):
        place(row, top[row].reshape(64, 2 * BREADTH))
        place(row + edge + height, bottom[row].reshape(64, 2 * BREADTH))
        return carry

    lax.fori_loop(0, edge, ends, 0)

    def one(row, keep):
        cells = parts[pl.ds(2 * row, 4)].reshape(1024, BREADTH)
        pre = dot(weight[...], cells)
        small = jnp.exp(-jnp.abs(pre))
        whole = 1.0 + small
        value = 0.3 * pre + 0.7 * (jnp.maximum(pre, 0.0) + jnp.log(whole))
        summed = jnp.sum(value.reshape(8, 32, BREADTH), axis=0) * 0.125
        at = first_ref[0] + row
        inside = jnp.logical_and(at >= 0, at < count_ref[0])
        pooled[row] = jnp.where(inside, summed, 0.0).astype(BF16)
        if keep:
            slope[row - 2] = 0.3 + 0.7 * (jnp.where(pre >= 0.0, 1.0, small) / whole)

    rows = pooled.shape[0]
    for row in (0, 1, rows - 2, rows - 1):
        one(row, False)

    def inner(row, carry):
        one(row, True)
        return carry

    lax.fori_loop(2, rows - 2, inner, 0, unroll=2)


def forward_three(below, own, above, cot, weight, grads, parts, shift):
    shift[...] = shifter()
    rows = own.shape[0]
    for plane, ref in enumerate((below, own, above)):

        def place(row, carry, plane=plane, ref=ref):
            block = ref[row]
            moved = dot(block, shift[...]).astype(BF16)
            at = plane * 32
            parts[row, at : at + 32, :] = moved[:, :BREADTH]
            parts[row, 96 + at : 96 + at + 32, :] = block
            parts[row, 192 + at : 192 + at + 32, :] = moved[:, BREADTH:]
            return carry

        lax.fori_loop(0, rows, place, 0, unroll=2)

    def one(row, carry):
        pre = dot(weight[...], parts[pl.ds(row, 3)].reshape(864, BREADTH))
        small = jnp.exp(-jnp.abs(pre))
        slope = 0.3 + 0.7 * (jnp.where(pre >= 0.0, 1.0, small) / (1.0 + small))
        grads[row] = (cot[row].astype(F32) * slope).astype(BF16)
        return carry

    lax.fori_loop(0, rows - 2, one, 0, unroll=2)


def filters_three(grads, parts, out):
    left = jnp.concatenate([grads[row] for row in range(2, 10)], axis=1)
    for off in range(3):
        right = jnp.concatenate([parts[row + off] for row in range(2, 10)], axis=1)
        out[off] = dot_nt(left, right)


def backward_three(first_ref, count_ref, below, own, above, slope, weight, grads, parts, shift):
    shift[...] = shifter()
    rows = own.shape[0]
    for plane, ref in enumerate((below, own, above)):

        def place(row, carry, plane=plane, ref=ref):
            block = ref[row]
            moved = dot(block, shift[...]).astype(BF16)
            at = plane * 64
            parts[row, at : at + 64, :] = moved[:, :BREADTH]
            parts[row, 192 + at : 192 + at + 64, :] = block
            parts[row, 384 + at : 384 + at + 64, :] = moved[:, BREADTH:]
            return carry

        lax.fori_loop(0, rows, place, 0, unroll=2)

    def one(row, carry):
        pool = dot(weight[...], parts[pl.ds(row, 3)].reshape(1728, BREADTH))
        at = first_ref[0] + row
        inside = jnp.logical_and(at >= 0, at < count_ref[0])
        pool = jnp.where(inside, pool, 0.0) * 0.125
        full = pool[None] * slope[row].reshape(8, 32, BREADTH)
        grads[row] = full.astype(BF16).reshape(256, BREADTH)
        return carry

    lax.fori_loop(0, rows - 2, one, 0, unroll=2)


def filters_two(grads, parts, out):
    left = jnp.concatenate([grads[row] for row in range(1, 9)], axis=1)
    blocks = []
    for off in range(4):
        right = jnp.concatenate([parts[2 * row + 4 + off] for row in range(1, 9)], axis=1)
        blocks.append(dot_nt(left, right))
    total = jnp.concatenate(
        [jnp.zeros((32, 256), F32)] * 3, axis=1
    )
    for phase in range(8):
        deep, high, wide = phase // 4, (phase // 2) % 2, phase % 2
        part = jnp.concatenate(
            [block[phase * 32 : phase * 32 + 32] for block in blocks[high : high + 3]], axis=1
        )
        move = (wide * 4 + deep) * 16
        if move:
            part = pltpu.roll(part, 768 - move, 1)
        total = total + part
    out[...] = total


def backward_two(own, below, above, weight, out, parts, shift, join):
    shift[...] = shifter()
    join[...] = joiner()

    def place(row, carry):
        for high in range(2):
            for deep in range(4):
                ref, at = ((below, 0), (own, 0), (own, 128), (above, 0))[deep]
                at = at + high * 64
                even = ref[row, at : at + 32, :]
                odd = ref[row, at + 32 : at + 64, :]
                left = dot(odd, shift[:, :BREADTH]).astype(BF16)
                right = dot(even, shift[:, BREADTH:]).astype(BF16)
                for part, block in enumerate((left, even, odd, right)):
                    to = part * 128 + deep * 32
                    parts[2 * row + high, to : to + 32, :] = block
        return carry

    lax.fori_loop(0, own.shape[0], place, 0)

    def one(row, carry):
        cells = dot(weight[...], parts[pl.ds(2 * row + 1, 4)].reshape(2048, BREADTH)).astype(BF16)
        both = jnp.concatenate([cells[:64], cells[64:]], axis=1)
        out[row] = dot(both, join[...]).astype(BF16)
        return carry

    lax.fori_loop(0, out.shape[0], one, 0, unroll=2)


def tap_choice(back):
    chosen = np.full((8, 64), 27, np.int32)
    for phase in range(8):
        deep, high, wide = phase // 4, (phase // 2) % 2, phase % 2
        for place in range(64):
            b, e, a = place // 16 - high, (place // 4) % 4 - wide, place % 4 - deep
            if min(a, b, e) >= 0 and max(a, b, e) <= 2:
                if back:
                    a, b, e = 2 - a, 2 - b, 2 - e
                chosen[phase, place] = a * 9 + b * 3 + e
    return chosen


def taps_two(weight, back):
    taps = weight.reshape(27, 32, 16)
    if back:
        taps = jnp.transpose(taps, (0, 2, 1))
    outs, ins = taps.shape[1:]
    pick = jnp.asarray(np.eye(28)[tap_choice(back)][..., :27], BF16)
    full = jnp.einsum("pkt,tfc->pfkc", pick, taps, preferred_element_type=F32).astype(BF16)
    if back:
        full = jnp.transpose(full.reshape(2, 2, 2, outs, 64 * ins), (2, 0, 1, 3, 4))
    return full.reshape(8 * outs, 64 * ins)


def shifted(axis, step):
    count = lax.axis_size(axis)
    return [(i, i + step) for i in range(count) if 0 <= i + step < count]


def neighbours(first, last, axis):
    return (
        lax.ppermute(last, axis, shifted(axis, 1)),
        lax.ppermute(first, axis, shifted(axis, -1)),
    )


def exchange(blocks, axis):
    return lax.all_to_all(blocks, axis, 0, 0, tiled=True)


def summed_parts(total, axis):
    return jnp.sum(exchange(total, axis), axis=0)


def gathered(block, axis):
    count = lax.axis_size(axis)
    return exchange(jnp.broadcast_to(block[None], (count,) + block.shape), axis)


def on_device(inputs, weight_two, weight_three, cotangent):
    groups = lax.axis_size("grp")
    slabs = lax.axis_size("depth")
    group = lax.axis_index("grp")
    chans, planes, height, breadth = inputs.shape
    cells = planes * slabs * height * groups * breadth
    pool_rows = height // 2
    count = jnp.full((1,), pool_rows * groups, jnp.int32)
    share = weight_three.shape[3]
    filters = share * groups

    own = jnp.transpose(inputs, (2, 1, 0, 3))
    below, above = neighbours(own[:, 0], own[:, 1], "depth")

    def edge(lo):
        return jnp.concatenate(
            [below[lo : lo + 7, None], own[lo : lo + 7], above[lo : lo + 7, None]], axis=1
        )

    top, bottom = neighbours(edge(0), edge(height - 7), "grp")

    padded = jnp.pad(cotangent[:, 0], ((0, 0), (2, 2), (0, 0)))
    rows_out = jnp.stack(
        [
            padded[:, pool_rows * to : pool_rows * to + pool_rows + 4].reshape(-1, BREADTH)
            for to in range(groups)
        ]
    )
    weights_out = jnp.broadcast_to(
        weight_three.reshape(1, -1, BREADTH), (groups, weight_three.size // BREADTH, BREADTH)
    )
    arrived = exchange(jnp.concatenate([rows_out, weights_out], axis=1), "grp")
    cut = share * (pool_rows + 4)
    cot = jnp.transpose(arrived[:, :cut].reshape(filters, pool_rows + 4, BREADTH), (1, 0, 2))
    taps = arrived[:, cut:].reshape(groups, 3, 3, 3, share, 32)
    weight_fwd = jnp.transpose(taps, (0, 4, 2, 3, 1, 5)).reshape(filters, 864)
    weight_back = jnp.transpose(
        taps[:, ::-1, ::-1, ::-1], (5, 2, 3, 1, 0, 4)
    ).reshape(32, 27 * filters)

    first = (pool_rows * group - 3).astype(jnp.int32).reshape(1)
    pooled, slope, parts_two = call(
        forward_two,
        [
            jax.ShapeDtypeStruct((pool_rows + 6, 32, BREADTH), BF16),
            jax.ShapeDtypeStruct((pool_rows + 2, 256, BREADTH), F32),
            jax.ShapeDtypeStruct((height + 14, 256, BREADTH), BF16),
        ],
        [pltpu.VMEM((2 * BREADTH, 4 * BREADTH), BF16)],
        (first, count, own, below, above, top, bottom, taps_two(weight_two, False)),
        2 * 14 * 256 * 1024 * 128,
        scalars=2,
    )

    pool_below, pool_above = neighbours(pooled, pooled, "depth")
    shift = pltpu.VMEM((BREADTH, 2 * BREADTH), BF16)
    grads, parts_three = call(
        forward_three,
        [
            jax.ShapeDtypeStruct((pool_rows + 4, filters, BREADTH), BF16),
            jax.ShapeDtypeStruct((pool_rows + 6, 288, BREADTH), BF16),
        ],
        [shift],
        (pool_below, pooled, pool_above, cot, weight_fwd),
        2 * 12 * 64 * 864 * 128,
    )

    grads_below, grads_above = neighbours(grads, grads, "depth")
    (local_three,) = call(
        filters_three,
        [jax.ShapeDtypeStruct((3, filters, 288), F32)],
        [],
        (grads, parts_three),
        2 * 8 * 64 * 864 * 128,
    )
    (grad_two,) = call(
        backward_three,
        [jax.ShapeDtypeStruct((pool_rows + 2, 256, BREADTH), BF16)],
        [pltpu.VMEM((pool_rows + 4, 576, BREADTH), BF16), shift],
        (first + 2, count, grads_below, grads, grads_above, slope, weight_back),
        2 * 10 * 32 * 1728 * 128,
        scalars=2,
    )

    two_below, two_above = neighbours(grad_two[:, :128], grad_two[:, 128:], "depth")
    (local_two,) = call(
        filters_two,
        [jax.ShapeDtypeStruct((32, 768), F32)],
        [],
        (grad_two, parts_two),
        2 * 8 * 256 * 1024 * 128,
    )
    (back,) = call(
        backward_two,
        [jax.ShapeDtypeStruct((pool_rows, 64, 2 * BREADTH), BF16)],
        [
            pltpu.VMEM((height + 4, 512, BREADTH), BF16),
            shift,
            pltpu.VMEM((2 * BREADTH, 2 * BREADTH), BF16),
        ],
        (grad_two, two_below, two_above, taps_two(weight_two, True)),
        2 * 8 * 128 * 2048 * 128,
    )
    input_grad = jnp.transpose(
        back.reshape(pool_rows, 2, 2, chans, breadth), (3, 1, 0, 2, 4)
    ).reshape(inputs.shape)

    three = jnp.transpose(
        local_three.reshape(3, groups, share, 3, 3, 32), (1, 4, 0, 3, 2, 5)
    ).reshape(groups, -1, BREADTH)
    two = jnp.transpose(
        local_two.reshape(32, 3, 4, 4, 16)[:, :, :3, :3], (3, 1, 2, 0, 4)
    ).reshape(-1, BREADTH)
    size_two = two.shape[0]
    piece = -(-size_two // groups)
    two = jnp.pad(two, ((0, piece * groups - size_two), (0, 0))).reshape(groups, piece, BREADTH)
    mine = summed_parts(jnp.concatenate([three, two], axis=1), "grp")
    mine = gathered(summed_parts(mine.reshape(slabs, -1), "depth"), "depth").reshape(-1, BREADTH)
    rows_three = three.shape[1]
    weight_grad_three = mine[:rows_three].reshape(3, 3, 3, share, 32) * (1.0 / math.sqrt(cells / 8))
    full = gathered(mine[rows_three:], "grp").reshape(-1, BREADTH)[:size_two]
    weight_grad_two = full.reshape(3, 3, 3, 32, 16) * (1.0 / math.sqrt(cells))
    return (input_grad, weight_grad_two, weight_grad_three)


def solution(mesh):
    placed = (
        P(None, "depth", "grp", None),
        P(),
        P(None, None, None, "grp", None),
        P("grp", "depth", None, None),
    )
    return jax.shard_map(
        on_device,
        mesh=mesh,
        in_specs=placed,
        out_specs=(P(None, "depth", "grp", None), P(), P(None, None, None, "grp", None)),
        check_vma=False,
    )
```

```python
import functools
import math

import jax
import jax.numpy as jnp
from jax import lax
from jax.experimental import pallas as pl
from jax.experimental.pallas import tpu as pltpu
from jax.sharding import PartitionSpec as P


F32 = jnp.float32
BF16 = jnp.bfloat16
BREADTH = 128


def call(kernel, outs, scratch, args, flops, scalars=0):
    specs = [pl.BlockSpec(memory_space=pltpu.SMEM)] * scalars
    specs += [pl.BlockSpec(memory_space=pltpu.VMEM)] * (len(args) - scalars)
    moved = sum(math.prod(a.shape) * a.dtype.itemsize for a in list(args) + list(outs))
    return pl.pallas_call(
        kernel,
        out_shape=outs,
        in_specs=specs,
        out_specs=[pl.BlockSpec(memory_space=pltpu.VMEM)] * len(outs),
        scratch_shapes=scratch,
        compiler_params=pltpu.CompilerParams(vmem_limit_bytes=16 * 1024 * 1024),
        cost_estimate=pl.CostEstimate(flops=flops, bytes_accessed=moved, transcendentals=0),
    )(*args)


def dot(left, right):
    return jnp.dot(left, right, preferred_element_type=F32)


def dot_nt(left, right):
    return lax.dot_general(left, right, (((1,), (1,)), ((), ())), preferred_element_type=F32)


def indicator(shape, test):
    row = lax.broadcasted_iota(jnp.int32, shape, 0)
    col = lax.broadcasted_iota(jnp.int32, shape, 1)
    return jnp.where(test(row, col), 1.0, 0.0).astype(BF16)


def splitter():
    def test(row, col):
        part, at = col // BREADTH, col % BREADTH
        return row == 2 * at + part - 1

    return indicator((2 * BREADTH, 4 * BREADTH), test)


def shifter():
    def test(row, col):
        part, at = col // BREADTH, col % BREADTH
        return row == at + 2 * part - 1

    return indicator((BREADTH, 2 * BREADTH), test)


def joiner():
    def test(row, col):
        return col == 2 * (row % BREADTH) + row // BREADTH

    return indicator((2 * BREADTH, 2 * BREADTH), test)


def weights_two(plain, turned, ahead, back):
    def blocks(source, outs, ins, flip):
        per = BREADTH // ins
        total = []
        for part in range(64 // per):
            summed = jnp.zeros((outs, BREADTH), F32)
            for at in range(per):
                place = part * per + at
                b, e, a = place // 16, (place // 4) % 4, place % 4
                if max(a, b, e) > 2:
                    continue
                if flip:
                    a, b, e = 2 - a, 2 - b, 2 - e
                spread = indicator((ins, BREADTH), lambda row, col: col == row + at * ins)
                summed = summed + dot(source[a * 9 + b * 3 + e], spread)
            total.append(summed)
        return jnp.concatenate(total, axis=1)

    def phases(out, base, outs, ins, row_of):
        for phase in range(8):
            deep, high, wide = phase // 4, (phase // 2) % 2, phase % 2
            move = (high * 16 + wide * 4 + deep) * ins
            full = pltpu.roll(base, move, 1) if move else base
            at = row_of(deep, high, wide) * outs
            out[at : at + outs, :] = full.astype(BF16)

    phases(ahead, blocks(plain, 32, 16, False), 32, 16, lambda d, h, w: d * 4 + h * 2 + w)
    phases(back, blocks(turned, 16, 32, True), 16, 32, lambda d, h, w: w * 4 + d * 2 + h)


def forward_two(first_ref, count_ref, own, below, above, top, bottom, weight, pooled, slope, parts, split):
    split[...] = splitter()
    edge = top.shape[0]
    height = own.shape[0]

    def place(row, many, block):
        cells = dot(block, split[...]).astype(BF16).reshape(many, 64, 4 * BREADTH)
        for part in range(4):
            to = part * 64
            parts[row : row + many, to : to + 64, :] = cells[:, :, part * BREADTH : (part + 1) * BREADTH]

    for row in range(0, height, 4):
        block = [ref[at] for at in range(row, row + 4) for ref in (below, own.at[:, 0], own.at[:, 1], above)]
        place(row + edge, 4, jnp.concatenate(block, axis=0))
    for ref, to in ((top, 0), (bottom, edge + height)):
        for row, many in ((0, 4), (4, edge - 4)):
            place(to + row, many, ref[row : row + many].reshape(many * 64, 2 * BREADTH))

    rows = pooled.shape[0]
    for row in range(0, rows, 2):
        cells = [parts[2 * at : 2 * at + 4].reshape(1024, BREADTH) for at in (row, row + 1)]
        pre = dot(weight[...], jnp.concatenate(cells, axis=1))
        small = jnp.exp(-jnp.abs(pre))
        whole = 1.0 + small
        value = 0.3 * pre + 0.7 * (jnp.maximum(pre, 0.0) + jnp.log(whole))
        summed = jnp.sum(value.reshape(8, 32, 2 * BREADTH), axis=0) * 0.125
        for off in range(2):
            at = first_ref[0] + row + off
            inside = jnp.logical_and(at >= 0, at < count_ref[0])
            half = summed[:, off * BREADTH : (off + 1) * BREADTH]
            pooled[row + off] = jnp.where(inside, half, 0.0).astype(BF16)
        if 2 <= row < rows - 2:
            rate = 0.3 + 0.7 * (jnp.where(pre >= 0.0, 1.0, small) / whole)
            slope[row - 2] = rate[:, :BREADTH]
            slope[row - 1] = rate[:, BREADTH:]


def place_shifted(refs, parts, shift, chans):
    span = 3 * chans
    rows = refs[0].shape[0]
    step = 256 // chans
    for plane, ref in enumerate(refs):
        at = plane * chans
        for row in range(0, rows, step):
            many = min(step, rows - row)
            block = ref[row : row + many]
            moved = dot(block.reshape(many * chans, BREADTH), shift[...]).astype(BF16)
            moved = moved.reshape(many, chans, 2 * BREADTH)
            parts[row : row + many, at : at + chans, :] = moved[:, :, :BREADTH]
            parts[row : row + many, span + at : span + at + chans, :] = block
            parts[row : row + many, 2 * span + at : 2 * span + at + chans, :] = moved[:, :, BREADTH:]


def side_by_side(parts, row, many, taken, step=1):
    size = taken * parts.shape[1]
    return jnp.concatenate(
        [parts[at * step : at * step + taken].reshape(size, BREADTH) for at in range(row, row + many)],
        axis=1,
    )


def forward_three(below, own, above, arrived, grads, parts, shift):
    shift[...] = shifter()
    place_shifted((below, own, above), parts, shift, 32)
    rows = grads.shape[0]
    weight = arrived[:, rows * BREADTH :][:, :864]
    for row in range(0, rows, 4):
        pre = dot(weight, side_by_side(parts, row, 4, 3))
        small = jnp.exp(-jnp.abs(pre))
        rate = 0.3 + 0.7 * (jnp.where(pre >= 0.0, 1.0, small) / (1.0 + small))
        full = arrived[:, row * BREADTH : (row + 4) * BREADTH].astype(F32) * rate
        for off in range(4):
            grads[row + off] = full[:, off * BREADTH : (off + 1) * BREADTH].astype(BF16)


def filters_three(grads, parts, arrived, out, back):
    rows = grads.shape[0]
    left = jnp.concatenate([grads[row] for row in range(2, rows - 2)], axis=1)
    out[:, :864] = dot_nt(left, side_by_side(parts, 2, rows - 4, 3)).astype(BF16)
    out[:, 864:] = jnp.zeros((out.shape[0], out.shape[1] - 864), BF16)
    weight = arrived[:, rows * BREADTH :].astype(F32)
    turned = jnp.transpose(jnp.concatenate([weight, weight], axis=0))
    lane = lax.broadcasted_iota(jnp.int32, (32, BREADTH), 1)
    for tap in range(0, 27, 2):
        one = turned[(26 - tap) * 32 : (27 - tap) * 32]
        if tap == 26:
            back[:, tap * 64 : tap * 64 + 64] = one[:, :64].astype(BF16)
        else:
            two = turned[(25 - tap) * 32 : (26 - tap) * 32]
            pair = jnp.where(lane < 64, one, two)
            back[:, tap * 64 : tap * 64 + 128] = pair.astype(BF16)


def backward_three(first_ref, count_ref, below, own, above, slope, weight, grads, parts, shift):
    shift[...] = shifter()
    place_shifted((below, own, above), parts, shift, 64)
    rows = grads.shape[0]
    for row in range(0, rows, 2):
        pool = dot(weight[...], side_by_side(parts, row, 2, 3)) * 0.125
        for off in range(2):
            at = first_ref[0] + row + off
            inside = jnp.logical_and(at >= 0, at < count_ref[0])
            half = jnp.where(inside, pool[:, off * BREADTH : (off + 1) * BREADTH], 0.0)
            full = half[None] * slope[row + off].reshape(8, 32, BREADTH)
            grads[row + off] = full.astype(BF16).reshape(256, BREADTH)


def filters_two(grads, parts, out):
    rows = grads.shape[0] - 2
    left = jnp.concatenate([grads[row] for row in range(1, rows + 1)], axis=1)
    blocks = []
    for off in range(4):
        right = jnp.concatenate([parts[2 * row + 4 + off] for row in range(1, rows + 1)], axis=1)
        blocks.append(dot_nt(left, right))
    total = jnp.zeros((32, 768), F32)
    for phase in range(8):
        deep, high, wide = phase // 4, (phase // 2) % 2, phase % 2
        part = jnp.concatenate(
            [block[phase * 32 : phase * 32 + 32] for block in blocks[high : high + 3]], axis=1
        )
        move = (wide * 4 + deep) * 16
        if move:
            part = pltpu.roll(part, 768 - move, 1)
        total = total + part
    for half in range(2):
        for piece in range(3):
            at = (half * 3 + piece) * BREADTH
            out[piece, half * 32 : half * 32 + 32, :] = total[:, at : at + BREADTH].astype(BF16)


def backward_two(own, below, above, weight, out, parts, shift, join):
    shift[...] = shifter()
    join[...] = joiner()
    for row in range(own.shape[0]):
        block = jnp.concatenate([below[row], own[row], above[row]], axis=0)
        moved = dot(block, shift[...]).astype(BF16)
        for high in range(2):
            for deep in range(4):
                at = deep * 128 + high * 64
                to = deep * 32
                both = 2 * row + high
                parts[both, to : to + 32, :] = moved[at + 32 : at + 64, :BREADTH]
                parts[both, 128 + to : 160 + to, :] = block[at : at + 32]
                parts[both, 256 + to : 288 + to, :] = block[at + 32 : at + 64]
                parts[both, 384 + to : 416 + to, :] = moved[at : at + 32, BREADTH:]
    for row in range(0, out.shape[0], 2):
        cells = [parts[2 * at + 1 : 2 * at + 5].reshape(2048, BREADTH) for at in (row, row + 1)]
        cells = dot(weight[...], jnp.concatenate(cells, axis=1)).astype(BF16)
        both = [
            jnp.concatenate([cells[:64, at : at + BREADTH], cells[64:, at : at + BREADTH]], axis=1)
            for at in (0, BREADTH)
        ]
        joined = dot(jnp.concatenate(both, axis=0), join[...]).astype(BF16)
        out[row] = joined[:64]
        out[row + 1] = joined[64:]


def spread_out(scale_two, scale_three, sums, two, three):
    for part in range(6):
        half, piece = part // 3, part % 3
        block = sums[piece, half * 32 : half * 32 + 32, :].astype(F32) * scale_two
        for at in range(8):
            b, e, a = part // 2, (part % 2) * 2 + at // 4, at % 4
            if max(a, e) <= 2:
                two[a * 9 + b * 3 + e] = block[:, at * 16 : at * 16 + 16]
    for part in range(7):
        block = sums[3, part * 8 : part * 8 + 8, :].astype(F32) * scale_three
        for at in range(4):
            tap = part * 4 + at
            if tap < 27:
                b, e, a = tap // 9, (tap // 3) % 3, tap % 3
                three[a * 9 + b * 3 + e] = block[:, at * 32 : at * 32 + 32]


def shifted(axis, step):
    count = lax.axis_size(axis)
    return [(i, i + step) for i in range(count) if 0 <= i + step < count]


def neighbours(first, last, axis):
    return (
        lax.ppermute(last, axis, shifted(axis, 1)),
        lax.ppermute(first, axis, shifted(axis, -1)),
    )


def exchange(blocks, axis):
    return lax.all_to_all(blocks, axis, 0, 0, tiled=True)


def gathered(block, axis):
    count = lax.axis_size(axis)
    return exchange(jnp.broadcast_to(block[None], (count,) + block.shape), axis)


def total_of(blocks):
    return jnp.sum(blocks.astype(F32), axis=0)


def on_device(inputs, weight_two, weight_three, cotangent):
    groups = lax.axis_size("grp")
    slabs = lax.axis_size("depth")
    group = lax.axis_index("grp")
    chans, planes, height, breadth = inputs.shape
    cells = planes * slabs * height * groups * breadth
    pool_rows = height // 2
    count = jnp.full((1,), pool_rows * groups, jnp.int32)
    share = weight_three.shape[3]
    filters = share * groups

    own = jnp.transpose(inputs, (2, 1, 0, 3))
    below, above = neighbours(own[:, 0], own[:, 1], "depth")

    def edge(lo):
        return jnp.concatenate(
            [below[lo : lo + 7, None], own[lo : lo + 7], above[lo : lo + 7, None]], axis=1
        )

    top, bottom = neighbours(edge(0), edge(height - 7), "grp")

    rows_out = jnp.pad(cotangent.reshape(share, -1), ((0, 0), (2 * BREADTH, 2 * BREADTH)))
    weight_out = jnp.transpose(weight_three, (3, 1, 2, 0, 4)).reshape(share, 864)
    weight_out = jnp.pad(weight_out, ((0, 0), (0, 32)))
    span = pool_rows * BREADTH
    arrived = exchange(
        jnp.stack(
            [
                jnp.concatenate(
                    [rows_out[:, span * to : span * (to + 1) + 4 * BREADTH], weight_out], axis=1
                )
                for to in range(groups)
            ]
        ),
        "grp",
    ).reshape(filters, -1)

    plain = weight_two.reshape(27, 32, 16)
    ahead, back = call(
        weights_two,
        [jax.ShapeDtypeStruct((256, 1024), BF16), jax.ShapeDtypeStruct((128, 2048), BF16)],
        [],
        (plain, jnp.transpose(plain, (0, 2, 1))),
        2 * 256 * 1024 * 128,
    )

    first = (pool_rows * group - 3).astype(jnp.int32).reshape(1)
    pooled, slope, parts_two = call(
        forward_two,
        [
            jax.ShapeDtypeStruct((pool_rows + 6, 32, BREADTH), BF16),
            jax.ShapeDtypeStruct((pool_rows + 2, 256, BREADTH), F32),
            jax.ShapeDtypeStruct((height + 14, 256, BREADTH), BF16),
        ],
        [pltpu.VMEM((2 * BREADTH, 4 * BREADTH), BF16)],
        (first, count, own, below, above, top, bottom, ahead),
        2 * 14 * 256 * 1024 * 128,
        scalars=2,
    )

    pool_below, pool_above = neighbours(pooled, pooled, "depth")
    shift = pltpu.VMEM((BREADTH, 2 * BREADTH), BF16)
    grads, parts_three = call(
        forward_three,
        [
            jax.ShapeDtypeStruct((pool_rows + 4, filters, BREADTH), BF16),
            jax.ShapeDtypeStruct((pool_rows + 6, 288, BREADTH), BF16),
        ],
        [shift],
        (pool_below, pooled, pool_above, arrived),
        2 * 12 * 64 * 864 * 128,
    )

    grads_below, grads_above = neighbours(grads, grads, "depth")
    local_three, weight_back = call(
        filters_three,
        [
            jax.ShapeDtypeStruct((filters, 1024), BF16),
            jax.ShapeDtypeStruct((32, 27 * filters), BF16),
        ],
        [],
        (grads, parts_three, arrived),
        2 * 8 * 64 * 864 * 128,
    )
    three = total_of(exchange(local_three.reshape(groups, share, 1024), "grp"))
    three = jnp.transpose(three.reshape(share, 8, BREADTH), (1, 0, 2)).reshape(1, -1, BREADTH)
    (grad_two,) = call(
        backward_three,
        [jax.ShapeDtypeStruct((pool_rows + 2, 256, BREADTH), BF16)],
        [pltpu.VMEM((pool_rows + 4, 576, BREADTH), BF16), shift],
        (first + 2, count, grads_below, grads, grads_above, slope, weight_back),
        2 * 10 * 32 * 1728 * 128,
        scalars=2,
    )

    (local_two,) = call(
        filters_two,
        [jax.ShapeDtypeStruct((3, 64, BREADTH), BF16)],
        [],
        (grad_two, parts_two),
        2 * 8 * 256 * 1024 * 128,
    )
    two_below, two_above = neighbours(grad_two[:, :128], grad_two[:, 128:], "depth")
    (cells_back,) = call(
        backward_two,
        [jax.ShapeDtypeStruct((pool_rows, 64, 2 * BREADTH), BF16)],
        [
            pltpu.VMEM((height + 4, 512, BREADTH), BF16),
            shift,
            pltpu.VMEM((2 * BREADTH, 2 * BREADTH), BF16),
        ],
        (grad_two, two_below, two_above, back),
        2 * 8 * 128 * 2048 * 128,
    )
    input_grad = jnp.transpose(
        cells_back.reshape(pool_rows, 2, 2, chans, breadth), (3, 1, 0, 2, 4)
    ).reshape(inputs.shape)

    sums = jnp.concatenate([local_two, three.astype(BF16)], axis=0)
    sums = jnp.transpose(sums.reshape(4, slabs, -1), (1, 0, 2))
    mine = total_of(exchange(sums, "depth"))
    both = total_of(gathered(mine.astype(BF16), "grp"))
    mine = jnp.concatenate([both[:3], mine[3:]], axis=0).astype(BF16)
    sums = jnp.transpose(gathered(mine, "depth"), (1, 0, 2)).reshape(4, 64, BREADTH)
    two, three = call(
        functools.partial(spread_out, 1.0 / math.sqrt(cells), 1.0 / math.sqrt(cells / 8)),
        [
            jax.ShapeDtypeStruct((27, 32, 16), F32),
            jax.ShapeDtypeStruct((27, share, 32), F32),
        ],
        [],
        (sums,),
        2 * 64 * 1024,
    )
    return (input_grad, two.reshape(weight_two.shape), three.reshape(weight_three.shape))


def solution(mesh):
    placed = (
        P(None, "depth", "grp", None),
        P(),
        P(None, None, None, "grp", None),
        P("grp", "depth", None, None),
    )
    return jax.shard_map(
        on_device,
        mesh=mesh,
        in_specs=placed,
        out_specs=(P(None, "depth", "grp", None), P(), P(None, None, None, "grp", None)),
        check_vma=False,
    )
```

```python
import functools
import math

import jax
import jax.numpy as jnp
from jax import lax
from jax.experimental import pallas as pl
from jax.experimental.pallas import tpu as pltpu
from jax.sharding import PartitionSpec as P


F32 = jnp.float32
BF16 = jnp.bfloat16
BREADTH = 128


def call(kernel, outs, scratch, args, flops):
    specs = [pl.BlockSpec(memory_space=pltpu.VMEM)] * len(args)
    moved = sum(math.prod(a.shape) * a.dtype.itemsize for a in list(args) + list(outs))
    return pl.pallas_call(
        kernel,
        out_shape=outs,
        in_specs=specs,
        out_specs=[pl.BlockSpec(memory_space=pltpu.VMEM)] * len(outs),
        scratch_shapes=scratch,
        compiler_params=pltpu.CompilerParams(vmem_limit_bytes=16 * 1024 * 1024),
        cost_estimate=pl.CostEstimate(flops=flops, bytes_accessed=moved, transcendentals=0),
    )(*args)


def dot(left, right):
    return jnp.dot(left, right, preferred_element_type=F32)


def dot_nt(left, right):
    return lax.dot_general(left, right, (((1,), (1,)), ((), ())), preferred_element_type=F32)


def indicator(shape, test):
    row = lax.broadcasted_iota(jnp.int32, shape, 0)
    col = lax.broadcasted_iota(jnp.int32, shape, 1)
    return jnp.where(test(row, col), 1.0, 0.0).astype(BF16)


def splitter():
    def test(row, col):
        part, at = col // BREADTH, col % BREADTH
        return row == 2 * at + part - 1

    return indicator((2 * BREADTH, 4 * BREADTH), test)


def shifter():
    def test(row, col):
        part, at = col // BREADTH, col % BREADTH
        return row == at + 2 * part - 1

    return indicator((BREADTH, 2 * BREADTH), test)


def joiner():
    def test(row, col):
        return col == 2 * (row % BREADTH) + row // BREADTH

    return indicator((2 * BREADTH, 2 * BREADTH), test)


def weights_two(plain, turned, ahead, back):
    def blocks(source, outs, ins, flip):
        per = BREADTH // ins
        total = []
        for part in range(64 // per):
            summed = jnp.zeros((outs, BREADTH), F32)
            for at in range(per):
                place = part * per + at
                b, e, a = place // 16, (place // 4) % 4, place % 4
                if max(a, b, e) > 2:
                    continue
                if flip:
                    a, b, e = 2 - a, 2 - b, 2 - e
                spread = indicator((ins, BREADTH), lambda row, col: col == row + at * ins)
                summed = summed + dot(source[a * 9 + b * 3 + e], spread)
            total.append(summed)
        return jnp.concatenate(total, axis=1)

    def phases(out, base, outs, ins, row_of):
        for phase in range(8):
            deep, high, wide = phase // 4, (phase // 2) % 2, phase % 2
            move = (high * 16 + wide * 4 + deep) * ins
            full = pltpu.roll(base, move, 1) if move else base
            at = row_of(deep, high, wide) * outs
            out[at : at + outs, :] = full.astype(BF16)

    phases(ahead, blocks(plain, 32, 16, False), 32, 16, lambda d, h, w: d * 4 + h * 2 + w)
    phases(back, blocks(turned, 16, 32, True), 16, 32, lambda d, h, w: w * 4 + d * 2 + h)


def inside(at, rows):
    return jnp.logical_and(at >= 0, at < rows * lax.axis_size("grp"))


def forward_two(own, below, above, top, bottom, weight, pooled, slope, parts, split):
    split[...] = splitter()
    first = pooled.shape[0] - 6
    first = first * lax.axis_index("grp") - 3
    edge = top.shape[0]
    height = own.shape[0]

    def place(row, many, block):
        cells = dot(block, split[...]).astype(BF16).reshape(many, 64, 4 * BREADTH)
        for part in range(4):
            to = part * 64
            parts[row : row + many, to : to + 64, :] = cells[:, :, part * BREADTH : (part + 1) * BREADTH]

    for ref, to in ((top, 0), (own, edge), (bottom, edge + height)):
        for row in range(0, ref.shape[0], 4):
            block = []
            for at in range(row, min(row + 4, ref.shape[0])):
                block += [below[to + at], ref[at, 0], ref[at, 1], above[to + at]]
            place(to + row, len(block) // 4, jnp.concatenate(block, axis=0))

    rows = pooled.shape[0]
    for row in range(0, rows, 2):
        cells = [parts[2 * at : 2 * at + 4].reshape(1024, BREADTH) for at in (row, row + 1)]
        pre = dot(weight[...], jnp.concatenate(cells, axis=1))
        small = jnp.exp(-jnp.abs(pre))
        whole = 1.0 + small
        value = 0.3 * pre + 0.7 * (jnp.maximum(pre, 0.0) + jnp.log(whole))
        summed = jnp.sum(value.reshape(8, 32, 2 * BREADTH), axis=0) * 0.125
        for off in range(2):
            half = summed[:, off * BREADTH : (off + 1) * BREADTH]
            kept = inside(first + row + off, rows - 6)
            pooled[row + off] = jnp.where(kept, half, 0.0).astype(BF16)
        if 2 <= row < rows - 2:
            rate = 0.3 + 0.7 * (jnp.where(pre >= 0.0, 1.0, small) / whole)
            slope[row - 2] = rate[:, :BREADTH]
            slope[row - 1] = rate[:, BREADTH:]


def place_shifted(refs, parts, shift, chans):
    span = len(refs) * chans
    rows = refs[0].shape[0]
    step = 256 // chans
    for plane, ref in enumerate(refs):
        at = plane * chans
        for row in range(0, rows, step):
            many = min(step, rows - row)
            block = ref[row : row + many]
            moved = dot(block.reshape(many * chans, BREADTH), shift[...]).astype(BF16)
            moved = moved.reshape(many, chans, 2 * BREADTH)
            parts[row : row + many, at : at + chans, :] = moved[:, :, :BREADTH]
            parts[row : row + many, span + at : span + at + chans, :] = block
            parts[row : row + many, 2 * span + at : 2 * span + at + chans, :] = moved[:, :, BREADTH:]


def side_by_side(parts, row, many, taken, step=1):
    size = taken * parts.shape[1]
    return jnp.concatenate(
        [parts[at * step : at * step + taken].reshape(size, BREADTH) for at in range(row, row + many)],
        axis=1,
    )


def pack(cot, taps, out):
    count, share, width = out.shape
    rows = cot.shape[0] // count
    extra = (width - 896) // BREADTH - rows
    blocks = []
    for part in range(7):
        piece = []
        for tap in range(part * 4, part * 4 + 4):
            at = (tap % 3) * 9 + (tap // 9) * 3 + (tap // 3) % 3
            piece.append(taps[at].astype(F32) if tap < 27 else jnp.zeros((share, 32), F32))
        blocks.append(jnp.concatenate(piece, axis=1).astype(BF16))
    for to in range(count):
        for row in range(rows + extra):
            at = rows * to - extra // 2 + row
            lane = row * BREADTH
            if 0 <= at < cot.shape[0]:
                out[to, :, lane : lane + BREADTH] = cot[at]
            else:
                out[to, :, lane : lane + BREADTH] = jnp.zeros((share, BREADTH), BF16)
        for part in range(7):
            lane = (rows + extra + part) * BREADTH
            out[to, :, lane : lane + BREADTH] = blocks[part]


def middle_three(below, own, above, arrived, grads, parts, down, same, up, shift, around, turned):
    shift[...] = shifter()
    place_shifted((below, own, above), parts, shift, 32)
    rows = grads.shape[0]
    span = rows * BREADTH
    weight = arrived[:, span:]
    for row in range(0, rows, 4):
        pre = dot(weight[:, :864], side_by_side(parts, row, 4, 3))
        small = jnp.exp(-jnp.abs(pre))
        rate = 0.3 + 0.7 * (jnp.where(pre >= 0.0, 1.0, small) / (1.0 + small))
        full = arrived[:, row * BREADTH : (row + 4) * BREADTH].astype(F32) * rate
        for off in range(4):
            grads[row + off] = full[:, off * BREADTH : (off + 1) * BREADTH].astype(BF16)
    weight = weight.astype(F32)
    flat = jnp.transpose(jnp.concatenate([weight, weight], axis=0))
    lane = lax.broadcasted_iota(jnp.int32, (32, BREADTH), 1)
    for plane in range(3):

        def tap(at, plane=plane):
            first = ((8 - at) * 3 + 2 - plane) * 32
            return flat[first : first + 32]

        to = plane * 32
        for at in range(0, 8, 2):
            pair = jnp.where(lane < 64, tap(at), tap(at + 1))
            turned[to : to + 32, at * 64 : at * 64 + 128] = pair.astype(BF16)
        turned[to : to + 32, 512:576] = tap(8)[:, :64].astype(BF16)
    place_shifted((grads,), around, shift, 64)
    for row in range(0, rows - 2, 2):
        pool = dot(turned[...], side_by_side(around, row, 2, 3))
        for off in range(2):
            half = pool[:, off * BREADTH : (off + 1) * BREADTH]
            up[row + off] = half[:32].astype(BF16)
            same[row + off] = half[32:64]
            down[row + off] = half[64:].astype(BF16)


def filters_three(grads, parts, out):
    rows = grads.shape[0]
    left = jnp.concatenate([grads[row] for row in range(2, rows - 2)], axis=1)
    full = dot_nt(left, side_by_side(parts, 2, rows - 4, 3))
    full = jnp.concatenate([full, jnp.zeros((full.shape[0], 160), F32)], axis=1)
    for half in range(2):
        for to in range(8):
            for part in range(4):
                lane = (half * 4 + part) * BREADTH
                at = to * 32 + part * 8
                out[half, at : at + 8, :] = full[to * 8 : to * 8 + 8, lane : lane + BREADTH]


def middle_two(below, own, above, slope, parts, three, low, high, keep, send):
    rows = own.shape[0] - 2
    first = rows * lax.axis_index("grp") - 1
    left = []
    for row in range(rows + 2):
        pool = own[row] + below[row].astype(F32) + above[row].astype(F32)
        pool = jnp.where(inside(first + row, rows), pool, 0.0) * 0.125
        full = pool[None] * slope[row].reshape(8, 32, BREADTH)
        full = full.astype(BF16).reshape(256, BREADTH)
        low[row] = full[:128]
        high[row] = full[128:]
        if 1 <= row <= rows:
            left.append(full)
    left = jnp.concatenate(left, axis=1)
    blocks = []
    for off in range(4):
        right = jnp.concatenate([parts[2 * row + 4 + off] for row in range(1, rows + 1)], axis=1)
        blocks.append(dot_nt(left, right))
    total = jnp.zeros((32, 768), F32)
    for phase in range(8):
        deep, tall, wide = phase // 4, (phase // 2) % 2, phase % 2
        part = jnp.concatenate(
            [block[phase * 32 : phase * 32 + 32] for block in blocks[tall : tall + 3]], axis=1
        )
        move = (wide * 4 + deep) * 16
        if move:
            part = pltpu.roll(part, 768 - move, 1)
        total = total + part
    slot = lax.broadcasted_iota(jnp.int32, (32, BREADTH), 1) // 16
    dense = []
    rest = jnp.zeros((32, BREADTH), F32)
    for off in range(3):
        one = total[:, off * 256 : off * 256 + 128]
        two = total[:, off * 256 + 128 : off * 256 + 256]
        one = jnp.where(slot == 3, pltpu.roll(two, 48, 1), one)
        dense.append(jnp.where(slot == 7, pltpu.roll(two, 96, 1), one))
        moved = pltpu.roll(two, 96 + off * 16, 1) if off != 2 else two
        rest = jnp.where(slot == off, moved, rest)
    dense.append(rest)
    second = jnp.bitwise_and(lax.axis_index("depth"), 1) != 0
    one = jnp.concatenate(dense[:2] + [three[0]], axis=0)
    two = jnp.concatenate(dense[2:] + [three[1]], axis=0)
    keep[...] = jnp.where(second, two, one)
    send[...] = jnp.where(second, one, two)


def slot_of(b, e, a):
    if e < 2:
        return b, e * 4 + a
    return ((b, 3), (b, 7), (3, b))[a]


def halved(bit, mine, came, keep, send):
    count = (mine.shape[0] - 64) // 32
    total = (mine[...].astype(F32) + came[...].astype(F32)).astype(BF16)
    keep[:64, :] = total[:64]
    send[:64, :] = total[:64]
    group = lax.axis_index("grp")
    on = jnp.bitwise_and(group, bit) != 0
    for at in range(count // 2):
        zero, one = 64 + 64 * at, 96 + 64 * at
        to = 64 + 32 * at
        first, second = total[zero : zero + 32], total[one : one + 32]
        keep[to : to + 32, :] = jnp.where(on, second, first)
        send[to : to + 32, :] = jnp.where(on, first, second)


def backward_two(below, low, high, above, weight, out, parts, shift, join):
    shift[...] = shifter()
    join[...] = joiner()
    for row in range(low.shape[0]):
        block = jnp.concatenate([below[row], low[row], high[row], above[row]], axis=0)
        moved = dot(block, shift[...]).astype(BF16)
        for tall in range(2):
            for deep in range(4):
                at = deep * 128 + tall * 64
                to = deep * 32
                both = 2 * row + tall
                parts[both, to : to + 32, :] = moved[at + 32 : at + 64, :BREADTH]
                parts[both, 128 + to : 160 + to, :] = block[at : at + 32]
                parts[both, 256 + to : 288 + to, :] = block[at + 32 : at + 64]
                parts[both, 384 + to : 416 + to, :] = moved[at : at + 32, BREADTH:]
    for row in range(0, out.shape[0], 2):
        cells = [parts[2 * at + 1 : 2 * at + 5].reshape(2048, BREADTH) for at in (row, row + 1)]
        cells = dot(weight[...], jnp.concatenate(cells, axis=1)).astype(BF16)
        both = [
            jnp.concatenate([cells[:64, at : at + BREADTH], cells[64:, at : at + BREADTH]], axis=1)
            for at in (0, BREADTH)
        ]
        joined = dot(jnp.concatenate(both, axis=0), join[...]).astype(BF16)
        out[row] = joined[:64]
        out[row + 1] = joined[64:]


def spread_out(scale_two, scale_three, mine, other, two, three):
    second = jnp.bitwise_and(lax.axis_index("depth"), 1) != 0
    one, another = mine[...], other[...]
    lower, upper = jnp.where(second, another, one), jnp.where(second, one, another)
    flat = jnp.transpose(jnp.concatenate([lower[:64], upper[:64]], axis=0) * scale_two)
    for tap in range(27):
        a, b, e = tap // 9, (tap // 3) % 3, tap % 3
        block, slot = slot_of(b, e, a)
        two[tap] = flat[slot * 16 : slot * 16 + 16, block * 32 : block * 32 + 32]
    for part in range(7):
        at = 64 + (part % 4) * 8
        block = (lower, upper)[part // 4][at : at + 8] * scale_three
        for at in range(4):
            tap = part * 4 + at
            if tap < 27:
                b, e, a = tap // 9, (tap // 3) % 3, tap % 3
                three[a * 9 + b * 3 + e] = block[:, at * 32 : at * 32 + 32]


def shifted(axis, step):
    count = lax.axis_size(axis)
    return [(i, i + step) for i in range(count) if 0 <= i + step < count]


def neighbours(first, last, axis):
    return (
        lax.ppermute(last, axis, shifted(axis, 1)),
        lax.ppermute(first, axis, shifted(axis, -1)),
    )


def exchange(blocks, axis):
    return lax.all_to_all(blocks, axis, 0, 0, tiled=True)


def traded(block, axis, reach):
    return lax.ppermute(block, axis, [(i, i ^ reach) for i in range(lax.axis_size(axis))])


def on_device(inputs, weight_two, weight_three, cotangent):
    groups = lax.axis_size("grp")
    slabs = lax.axis_size("depth")
    chans, planes, height, breadth = inputs.shape
    cells = planes * slabs * height * groups * breadth
    pool_rows = height // 2
    share = weight_three.shape[3]
    filters = share * groups

    own = jnp.transpose(inputs, (2, 1, 0, 3))
    own, cotangent = lax.optimization_barrier((own, cotangent))
    top, bottom = neighbours(own[:7], own[height - 7 :], "grp")

    (packed,) = call(
        pack,
        [jax.ShapeDtypeStruct((groups, share, (pool_rows + 4) * BREADTH + 896), BF16)],
        [],
        (jnp.transpose(cotangent[:, 0], (1, 0, 2)), weight_three.reshape(27, share, 32)),
        2 * 64 * 1024,
    )
    arrived = exchange(packed, "grp").reshape(filters, -1)

    def whole(plane):
        return jnp.concatenate([top[:, plane], own[:, plane], bottom[:, plane]], axis=0)

    below, above = neighbours(whole(0), whole(1), "depth")

    plain = weight_two.reshape(27, 32, 16)
    ahead, back = call(
        weights_two,
        [jax.ShapeDtypeStruct((256, 1024), BF16), jax.ShapeDtypeStruct((128, 2048), BF16)],
        [],
        (plain, jnp.transpose(plain, (0, 2, 1))),
        2 * 256 * 1024 * 128,
    )

    pooled, slope, parts_two = call(
        forward_two,
        [
            jax.ShapeDtypeStruct((pool_rows + 6, 32, BREADTH), BF16),
            jax.ShapeDtypeStruct((pool_rows + 2, 256, BREADTH), F32),
            jax.ShapeDtypeStruct((height + 14, 256, BREADTH), BF16),
        ],
        [pltpu.VMEM((2 * BREADTH, 4 * BREADTH), BF16)],
        (own, below, above, top, bottom, ahead),
        2 * 14 * 256 * 1024 * 128,
    )

    pool_below, pool_above = neighbours(pooled, pooled, "depth")
    shift = pltpu.VMEM((BREADTH, 2 * BREADTH), BF16)
    terms = jax.ShapeDtypeStruct((pool_rows + 2, 32, BREADTH), BF16)
    grads, parts_three, down, same, up = call(
        middle_three,
        [
            jax.ShapeDtypeStruct((pool_rows + 4, filters, BREADTH), BF16),
            jax.ShapeDtypeStruct((pool_rows + 6, 288, BREADTH), BF16),
            terms,
            jax.ShapeDtypeStruct(terms.shape, F32),
            terms,
        ],
        [
            shift,
            pltpu.VMEM((pool_rows + 4, 3 * filters, BREADTH), BF16),
            pltpu.VMEM((96, 9 * filters), BF16),
        ],
        (pool_below, pooled, pool_above, arrived),
        2 * 12 * 64 * 864 * 128 * 2,
    )

    terms_below, terms_above = neighbours(down, up, "depth")
    (local_three,) = call(
        filters_three,
        [jax.ShapeDtypeStruct((2, groups * 32, BREADTH), F32)],
        [],
        (grads, parts_three),
        2 * 8 * 64 * 864 * 128,
    )
    halves = jax.ShapeDtypeStruct((64 + groups * 32, BREADTH), F32)
    plane = jax.ShapeDtypeStruct((pool_rows + 2, 128, BREADTH), BF16)
    low, high, keep, send = call(
        middle_two,
        [plane, plane, halves, halves],
        [],
        (terms_below, same, terms_above, slope, parts_two, local_three),
        2 * 8 * 256 * 1024 * 128,
    )

    came = traded(send, "depth", 1)
    two_below, two_above = neighbours(low, high, "depth")
    reach = 1
    while reach < groups:
        half = jax.ShapeDtypeStruct(((keep.shape[0] - 64) // 2 + 64, BREADTH), BF16)
        keep, send = call(
            functools.partial(halved, reach), [half, half], [], (keep, came), 1024 * 1024
        )
        if reach == 2:
            send, two_below, two_above = lax.optimization_barrier((send, two_below, two_above))
        came = traded(send, "grp", reach)
        reach *= 2
    mine = keep.astype(F32) + came.astype(F32)
    for reach in [slabs // 2] + [2**at for at in range(1, slabs.bit_length() - 2)]:
        mine = mine.astype(BF16)
        mine = mine.astype(F32) + traded(mine, "depth", reach).astype(F32)
    other = traded(mine, "depth", 1)
    two, three = call(
        functools.partial(spread_out, 1.0 / math.sqrt(cells), 1.0 / math.sqrt(cells / 8)),
        [
            jax.ShapeDtypeStruct((27, 16, 32), F32),
            jax.ShapeDtypeStruct((27, share, 32), F32),
        ],
        [],
        (mine, other),
        2 * 64 * 1024,
    )

    (cells_back,) = call(
        backward_two,
        [jax.ShapeDtypeStruct((pool_rows, 64, 2 * BREADTH), BF16)],
        [
            pltpu.VMEM((height + 4, 512, BREADTH), BF16),
            shift,
            pltpu.VMEM((2 * BREADTH, 2 * BREADTH), BF16),
        ],
        (two_below, low, high, two_above, back),
        2 * 8 * 128 * 2048 * 128,
    )
    input_grad = jnp.transpose(
        cells_back.reshape(pool_rows, 2, 2, chans, breadth), (3, 1, 0, 2, 4)
    ).reshape(inputs.shape)
    weight_grad_two = jnp.transpose(two, (0, 2, 1)).reshape(weight_two.shape)
    return (input_grad, weight_grad_two, three.reshape(weight_three.shape))


def solution(mesh):
    placed = (
        P(None, "depth", "grp", None),
        P(),
        P(None, None, None, "grp", None),
        P("grp", "depth", None, None),
    )
    return jax.shard_map(
        on_device,
        mesh=mesh,
        in_specs=placed,
        out_specs=(P(None, "depth", "grp", None), P(), P(None, None, None, "grp", None)),
        check_vma=False,
    )
```

```python
import functools
import math

import jax
import jax.numpy as jnp
from jax import lax
from jax.experimental import pallas as pl
from jax.experimental.pallas import tpu as pltpu
from jax.sharding import PartitionSpec as P


F32 = jnp.float32
BF16 = jnp.bfloat16
BREADTH = 128
DEPTH = ("yl", "z", "core")
GROUP = ("yh", "x")
NEAR = ("yl", "core", "yh", "x")


def axis_count(names):
    return math.prod(lax.axis_size(name) for name in names)


def group_index():
    return lax.axis_index("yh") * lax.axis_size("x") + lax.axis_index("x")


def call(kernel, outs, scratch, args, flops):
    specs = [pl.BlockSpec(memory_space=pltpu.VMEM)] * len(args)
    moved = sum(math.prod(a.shape) * a.dtype.itemsize for a in list(args) + list(outs))
    return pl.pallas_call(
        kernel,
        out_shape=outs,
        in_specs=specs,
        out_specs=[pl.BlockSpec(memory_space=pltpu.VMEM)] * len(outs),
        scratch_shapes=scratch,
        compiler_params=pltpu.CompilerParams(vmem_limit_bytes=16 * 1024 * 1024),
        cost_estimate=pl.CostEstimate(flops=flops, bytes_accessed=moved, transcendentals=0),
    )(*args)


def dot(left, right):
    return jnp.dot(left, right, preferred_element_type=F32)


def dot_nt(left, right):
    return lax.dot_general(left, right, (((1,), (1,)), ((), ())), preferred_element_type=F32)


def dot_tn(left, right):
    return lax.dot_general(left, right, (((0,), (0,)), ((), ())), preferred_element_type=F32)


def indicator(shape, test):
    row = lax.broadcasted_iota(jnp.int32, shape, 0)
    col = lax.broadcasted_iota(jnp.int32, shape, 1)
    return jnp.where(test(row, col), 1.0, 0.0).astype(BF16)


def splitter():
    def test(row, col):
        part, at = col // BREADTH, col % BREADTH
        return row == 2 * at + part - 1

    return indicator((2 * BREADTH, 4 * BREADTH), test)


def shifter():
    def test(row, col):
        part, at = col // BREADTH, col % BREADTH
        return row == at + 2 * part - 1

    return indicator((BREADTH, 2 * BREADTH), test)


def joiner():
    def test(row, col):
        return col == 2 * (row % BREADTH) + row // BREADTH

    return indicator((2 * BREADTH, 2 * BREADTH), test)


def weights_two(out, turned, flip):
    outs, ins = (16, 32) if flip else (32, 16)
    per = BREADTH // ins
    total = []
    for part in range(64 // per):
        summed = jnp.zeros((outs, BREADTH), F32)
        for at in range(per):
            place = part * per + at
            b, e, a = place // 16, (place // 4) % 4, place % 4
            if max(a, b, e) > 2:
                continue
            if flip:
                a, b, e = 2 - a, 2 - b, 2 - e
            spread = indicator((ins, BREADTH), lambda row, col: col == row + at * ins)
            tap = turned[a * 9 + b * 3 + e]
            summed = summed + (dot(tap, spread) if flip else dot_tn(tap, spread))
        total.append(summed)
    base = jnp.concatenate(total, axis=1)
    for phase in range(8):
        deep, high, wide = phase // 4, (phase // 2) % 2, phase % 2
        move = (high * 16 + wide * 4 + deep) * ins
        full = pltpu.roll(base, move, 1) if move else base
        at = (wide * 4 + deep * 2 + high if flip else phase) * outs
        out[at : at + outs, :] = full.astype(BF16)


def weights_ahead(turned, out):
    weights_two(out, turned, False)


def inside(at, rows):
    return jnp.logical_and(at >= 0, at < rows * axis_count(GROUP))


def forward_two(own, below, above, top, bottom, weight, pooled, slope, parts, split):
    split[...] = splitter()
    first = pooled.shape[0] - 6
    first = first * group_index() - 3
    edge = top.shape[0]
    height = own.shape[0]

    def place(row, many, block):
        cells = dot(block, split[...]).astype(BF16).reshape(many, 64, 4 * BREADTH)
        for part in range(4):
            to = part * 64
            parts[row : row + many, to : to + 64, :] = cells[:, :, part * BREADTH : (part + 1) * BREADTH]

    for ref, to in ((top, 0), (own, edge), (bottom, edge + height)):
        for row in range(0, ref.shape[0], 4):
            block = []
            for at in range(row, min(row + 4, ref.shape[0])):
                block += [below[to + at], ref[at, 0], ref[at, 1], above[to + at]]
            place(to + row, len(block) // 4, jnp.concatenate(block, axis=0))

    rows = pooled.shape[0]
    for row in range(0, rows, 2):
        cells = [parts[2 * at : 2 * at + 4].reshape(1024, BREADTH) for at in (row, row + 1)]
        pre = dot(weight[...], jnp.concatenate(cells, axis=1))
        small = jnp.exp(-jnp.abs(pre))
        whole = 1.0 + small
        value = 0.3 * pre + 0.7 * (jnp.maximum(pre, 0.0) + jnp.log(whole))
        summed = jnp.sum(value.reshape(8, 32, 2 * BREADTH), axis=0) * 0.125
        for off in range(2):
            half = summed[:, off * BREADTH : (off + 1) * BREADTH]
            kept = inside(first + row + off, rows - 6)
            pooled[row + off] = jnp.where(kept, half, 0.0).astype(BF16)
        if 2 <= row < rows - 2:
            rate = 0.3 + 0.7 * (jnp.where(pre >= 0.0, 1.0, small) / whole)
            slope[row - 2] = rate[:, :BREADTH]
            slope[row - 1] = rate[:, BREADTH:]


def place_shifted(refs, parts, shift, chans):
    span = len(refs) * chans
    rows = refs[0].shape[0]
    step = 256 // chans
    for plane, ref in enumerate(refs):
        at = plane * chans
        for row in range(0, rows, step):
            many = min(step, rows - row)
            block = ref[row : row + many]
            moved = dot(block.reshape(many * chans, BREADTH), shift[...]).astype(BF16)
            moved = moved.reshape(many, chans, 2 * BREADTH)
            parts[row : row + many, at : at + chans, :] = moved[:, :, :BREADTH]
            parts[row : row + many, span + at : span + at + chans, :] = block
            parts[row : row + many, 2 * span + at : 2 * span + at + chans, :] = moved[:, :, BREADTH:]


def side_by_side(parts, row, many, taken, step=1):
    size = taken * parts.shape[1]
    return jnp.concatenate(
        [parts[at * step : at * step + taken].reshape(size, BREADTH) for at in range(row, row + many)],
        axis=1,
    )


def pack(cot, taps, out):
    count, share, width = out.shape
    rows = cot.shape[0] // count
    extra = (width - 896) // BREADTH - rows
    blocks = []
    for part in range(7):
        piece = []
        for tap in range(part * 4, part * 4 + 4):
            at = (tap % 3) * 9 + (tap // 9) * 3 + (tap // 3) % 3
            piece.append(taps[at].astype(F32) if tap < 27 else jnp.zeros((share, 32), F32))
        blocks.append(jnp.concatenate(piece, axis=1).astype(BF16))
    for to in range(count):
        for row in range(rows + extra):
            at = rows * to - extra // 2 + row
            lane = row * BREADTH
            if 0 <= at < cot.shape[0]:
                out[to, :, lane : lane + BREADTH] = cot[at]
            else:
                out[to, :, lane : lane + BREADTH] = jnp.zeros((share, BREADTH), BF16)
        for part in range(7):
            lane = (rows + extra + part) * BREADTH
            out[to, :, lane : lane + BREADTH] = blocks[part]


def middle_three(below, own, above, arrived, grads, parts, down, same, up, shift, around, turned):
    shift[...] = shifter()
    place_shifted((below, own, above), parts, shift, 32)
    rows = grads.shape[0]
    span = rows * BREADTH
    weight = arrived[:, span:]
    for row in range(0, rows, 4):
        pre = dot(weight[:, :864], side_by_side(parts, row, 4, 3))
        small = jnp.exp(-jnp.abs(pre))
        rate = 0.3 + 0.7 * (jnp.where(pre >= 0.0, 1.0, small) / (1.0 + small))
        full = arrived[:, row * BREADTH : (row + 4) * BREADTH].astype(F32) * rate
        for off in range(4):
            grads[row + off] = full[:, off * BREADTH : (off + 1) * BREADTH].astype(BF16)
    weight = weight.astype(F32)
    flat = jnp.transpose(jnp.concatenate([weight, weight], axis=0))
    lane = lax.broadcasted_iota(jnp.int32, (32, BREADTH), 1)
    for plane in range(3):

        def tap(at, plane=plane):
            first = ((8 - at) * 3 + 2 - plane) * 32
            return flat[first : first + 32]

        to = plane * 32
        for at in range(0, 8, 2):
            pair = jnp.where(lane < 64, tap(at), tap(at + 1))
            turned[to : to + 32, at * 64 : at * 64 + 128] = pair.astype(BF16)
        turned[to : to + 32, 512:576] = tap(8)[:, :64].astype(BF16)
    place_shifted((grads,), around, shift, 64)
    for row in range(0, rows - 2, 2):
        pool = dot(turned[...], side_by_side(around, row, 2, 3))
        for off in range(2):
            half = pool[:, off * BREADTH : (off + 1) * BREADTH]
            up[row + off] = half[:32].astype(BF16)
            same[row + off] = half[32:64]
            down[row + off] = half[64:].astype(BF16)


def filters_three(grads, parts, out):
    rows = grads.shape[0]
    left = jnp.concatenate([grads[row] for row in range(2, rows - 2)], axis=1)
    full = dot_nt(left, side_by_side(parts, 2, rows - 4, 3))
    out[:, :864] = full
    out[:, 864:] = jnp.zeros((full.shape[0], 160), F32)


def middle_two(below, own, above, slope, parts, three, low, high, lines):
    rows = own.shape[0] - 2
    first = rows * group_index() - 1
    left = []
    for row in range(rows + 2):
        pool = own[row] + below[row].astype(F32) + above[row].astype(F32)
        pool = jnp.where(inside(first + row, rows), pool, 0.0) * 0.125
        full = pool[None] * slope[row].reshape(8, 32, BREADTH)
        full = full.astype(BF16).reshape(256, BREADTH)
        low[row] = full[:128]
        high[row] = full[128:]
        if 1 <= row <= rows:
            left.append(full)
    left = jnp.concatenate(left, axis=1)
    blocks = []
    for off in range(4):
        right = jnp.concatenate([parts[2 * row + 4 + off] for row in range(1, rows + 1)], axis=1)
        blocks.append(dot_nt(left, right))
    total = jnp.zeros((32, 768), F32)
    for phase in range(8):
        deep, tall, wide = phase // 4, (phase // 2) % 2, phase % 2
        part = jnp.concatenate(
            [block[phase * 32 : phase * 32 + 32] for block in blocks[tall : tall + 3]], axis=1
        )
        move = (wide * 4 + deep) * 16
        if move:
            part = pltpu.roll(part, 768 - move, 1)
        total = total + part
    slot = lax.broadcasted_iota(jnp.int32, (32, BREADTH), 1) // 16
    dense = []
    rest = jnp.zeros((32, BREADTH), F32)
    for off in range(3):
        one = total[:, off * 256 : off * 256 + 128]
        two = total[:, off * 256 + 128 : off * 256 + 256]
        one = jnp.where(slot == 3, pltpu.roll(two, 48, 1), one)
        dense.append(jnp.where(slot == 7, pltpu.roll(two, 96, 1), one))
        moved = pltpu.roll(two, 96 + off * 16, 1) if off != 2 else two
        rest = jnp.where(slot == off, moved, rest)
    dense.append(rest)
    for to in range(32):
        quarter, group = to // 8, to % 8
        for part in range(2):
            lane = (quarter * 2 + part) * BREADTH
            block = three[group * 8 : group * 8 + 8, lane : lane + BREADTH]
            lines[to, part * 8 : part * 8 + 8, :] = block
        for block in range(4):
            lines[to, 16 + block : 17 + block, :] = dense[block][to : to + 1]


def slot_of(b, e, a):
    if e < 2:
        return b, e * 4 + a
    return ((b, 3), (b, 7), (3, b))[a]


def backward_two(below, low, high, above, turned, out, parts, shift, join, weight):
    weights_two(weight, turned, True)
    shift[...] = shifter()
    join[...] = joiner()
    for row in range(low.shape[0]):
        block = jnp.concatenate([below[row], low[row], high[row], above[row]], axis=0)
        moved = dot(block, shift[...]).astype(BF16)
        for tall in range(2):
            for deep in range(4):
                at = deep * 128 + tall * 64
                to = deep * 32
                both = 2 * row + tall
                parts[both, to : to + 32, :] = moved[at + 32 : at + 64, :BREADTH]
                parts[both, 128 + to : 160 + to, :] = block[at : at + 32]
                parts[both, 256 + to : 288 + to, :] = block[at + 32 : at + 64]
                parts[both, 384 + to : 416 + to, :] = moved[at : at + 32, BREADTH:]
    for row in range(0, out.shape[0], 2):
        cells = [parts[2 * at + 1 : 2 * at + 5].reshape(2048, BREADTH) for at in (row, row + 1)]
        cells = dot(weight[...], jnp.concatenate(cells, axis=1)).astype(BF16)
        both = [
            jnp.concatenate([cells[:64, at : at + BREADTH], cells[64:, at : at + BREADTH]], axis=1)
            for at in (0, BREADTH)
        ]
        joined = dot(jnp.concatenate(both, axis=0), join[...]).astype(BF16)
        out[row] = joined[:64]
        out[row + 1] = joined[64:]


def spread_out(scale_two, scale_three, lines, two, three):
    for block in range(4):
        rows = [lines[at, 16 + block : 17 + block, :].astype(F32) for at in range(32)]
        flat = jnp.transpose(jnp.concatenate(rows * 4, axis=0) * scale_two)
        for tap in range(27):
            a, b, e = tap // 9, (tap // 3) % 3, tap % 3
            where, slot = slot_of(b, e, a)
            if where == block:
                two[tap] = flat[slot * 16 : slot * 16 + 16, :32]
    for part in range(7):
        at = (part // 2) * 8 + group_index()
        block = lines[at, (part % 2) * 8 : (part % 2) * 8 + 8, :].astype(F32) * scale_three
        for at in range(4):
            tap = part * 4 + at
            if tap < 27:
                b, e, a = tap // 9, (tap // 3) % 3, tap % 3
                three[a * 9 + b * 3 + e] = block[:, at * 32 : at * 32 + 32]


def shifted(axis, step):
    count = axis_count(axis)
    return [(i, i + step) for i in range(count) if 0 <= i + step < count]


def neighbours(first, last, axis):
    return (
        lax.ppermute(last, axis, shifted(axis, 1)),
        lax.ppermute(first, axis, shifted(axis, -1)),
    )


def exchange(blocks, axis):
    return lax.all_to_all(blocks, axis, 0, 0, tiled=True)


def total_of(blocks):
    return jnp.sum(blocks.astype(F32), axis=0).astype(BF16)


def copied(block, names):
    return jnp.broadcast_to(block[None], (axis_count(names),) + block.shape)


def on_device(inputs, weight_two, weight_three, cotangent):
    groups = axis_count(GROUP)
    slabs = axis_count(DEPTH)
    chans, planes, height, breadth = inputs.shape
    cells = planes * slabs * height * groups * breadth
    pool_rows = height // 2
    share = weight_three.shape[3]
    filters = share * groups

    own = jnp.transpose(inputs, (2, 1, 0, 3))
    own, cotangent = lax.optimization_barrier((own, cotangent))
    top, bottom = neighbours(own[:7], own[height - 7 :], GROUP)

    (packed,) = call(
        pack,
        [jax.ShapeDtypeStruct((groups, share, (pool_rows + 4) * BREADTH + 896), BF16)],
        [],
        (jnp.transpose(cotangent[:, 0], (1, 0, 2)), weight_three.reshape(27, share, 32)),
        2 * 64 * 1024,
    )
    arrived = exchange(packed, GROUP).reshape(filters, -1)

    def whole(plane):
        return jnp.concatenate([top[:, plane], own[:, plane], bottom[:, plane]], axis=0)

    below, above = neighbours(whole(0), whole(1), DEPTH)

    turned = jnp.transpose(weight_two.reshape(27, 32, 16), (0, 2, 1))
    (ahead,) = call(
        weights_ahead,
        [jax.ShapeDtypeStruct((256, 1024), BF16)],
        [],
        (turned,),
        2 * 256 * 1024 * 128,
    )
    ahead, arrived = lax.optimization_barrier((ahead, arrived))

    pooled, slope, parts_two = call(
        forward_two,
        [
            jax.ShapeDtypeStruct((pool_rows + 6, 32, BREADTH), BF16),
            jax.ShapeDtypeStruct((pool_rows + 2, 256, BREADTH), F32),
            jax.ShapeDtypeStruct((height + 14, 256, BREADTH), BF16),
        ],
        [pltpu.VMEM((2 * BREADTH, 4 * BREADTH), BF16)],
        (own, below, above, top, bottom, ahead),
        2 * 14 * 256 * 1024 * 128,
    )

    pool_below, pool_above = neighbours(pooled, pooled, DEPTH)
    shift = pltpu.VMEM((BREADTH, 2 * BREADTH), BF16)
    terms = jax.ShapeDtypeStruct((pool_rows + 2, 32, BREADTH), BF16)
    grads, parts_three, down, same, up = call(
        middle_three,
        [
            jax.ShapeDtypeStruct((pool_rows + 4, filters, BREADTH), BF16),
            jax.ShapeDtypeStruct((pool_rows + 6, 288, BREADTH), BF16),
            terms,
            jax.ShapeDtypeStruct(terms.shape, F32),
            terms,
        ],
        [
            shift,
            pltpu.VMEM((pool_rows + 4, 3 * filters, BREADTH), BF16),
            pltpu.VMEM((96, 9 * filters), BF16),
        ],
        (pool_below, pooled, pool_above, arrived),
        2 * 12 * 64 * 864 * 128 * 2,
    )

    terms_below, terms_above = neighbours(down, up, DEPTH)
    (local_three,) = call(
        filters_three,
        [jax.ShapeDtypeStruct((filters, 1024), F32)],
        [],
        (grads, parts_three),
        2 * 8 * 64 * 864 * 128,
    )
    plane = jax.ShapeDtypeStruct((pool_rows + 2, 128, BREADTH), BF16)
    low, high, lines = call(
        middle_two,
        [plane, plane, jax.ShapeDtypeStruct((32, 20, BREADTH), F32)],
        [],
        (terms_below, same, terms_above, slope, parts_two, local_three),
        2 * 8 * 256 * 1024 * 128,
    )

    two_below, two_above = neighbours(low, high, DEPTH)
    lines = lines.astype(BF16).reshape(32, 5, 4, BREADTH)
    lines = total_of(exchange(lines, NEAR))
    lines = total_of(exchange(copied(lines, ("z",)), "z"))
    lines = exchange(copied(lines, NEAR), NEAR).reshape(32, 20, BREADTH)
    two, three = call(
        functools.partial(spread_out, 1.0 / math.sqrt(cells), 1.0 / math.sqrt(cells / 8)),
        [
            jax.ShapeDtypeStruct((27, 16, 32), F32),
            jax.ShapeDtypeStruct((27, share, 32), F32),
        ],
        [],
        (lines.astype(F32),),
        2 * 64 * 1024,
    )

    (cells_back,) = call(
        backward_two,
        [jax.ShapeDtypeStruct((pool_rows, 64, 2 * BREADTH), BF16)],
        [
            pltpu.VMEM((height + 4, 512, BREADTH), BF16),
            shift,
            pltpu.VMEM((2 * BREADTH, 2 * BREADTH), BF16),
            pltpu.VMEM((128, 2048), BF16),
        ],
        (two_below, low, high, two_above, turned),
        2 * 8 * 128 * 2048 * 128,
    )
    input_grad = jnp.transpose(
        cells_back.reshape(pool_rows, 2, 2, chans, breadth), (3, 1, 0, 2, 4)
    ).reshape(inputs.shape)
    weight_grad_two = jnp.transpose(two, (0, 2, 1)).reshape(weight_two.shape)
    return (input_grad, weight_grad_two, three.reshape(weight_three.shape))


def solution(mesh):
    parts = jax.sharding.Mesh(mesh.devices.reshape(2, 16, 2, 2, 4), DEPTH + GROUP)
    placed = (
        P(None, DEPTH, GROUP, None),
        P(),
        P(None, None, None, GROUP, None),
        P(GROUP, DEPTH, None, None),
    )
    return jax.shard_map(
        on_device,
        mesh=parts,
        in_specs=placed,
        out_specs=(P(None, DEPTH, GROUP, None), P(), P(None, None, None, GROUP, None)),
        check_vma=False,
    )
```

```python
import functools
import math

import jax
import jax.numpy as jnp
from jax import lax
from jax.experimental import pallas as pl
from jax.experimental.pallas import tpu as pltpu
from jax.sharding import PartitionSpec as P


F32 = jnp.float32
BF16 = jnp.bfloat16
BREADTH = 128
DEPTH = ("yl", "z", "core")
GROUP = ("yh", "x")
NEAR = ("yl", "core", "yh", "x")


def axis_count(names):
    return math.prod(lax.axis_size(name) for name in names)


def group_index():
    return lax.axis_index("yh") * lax.axis_size("x") + lax.axis_index("x")


def call(kernel, outs, scratch, args, flops):
    specs = [pl.BlockSpec(memory_space=pltpu.VMEM)] * len(args)
    moved = sum(math.prod(a.shape) * a.dtype.itemsize for a in list(args) + list(outs))
    return pl.pallas_call(
        kernel,
        out_shape=outs,
        in_specs=specs,
        out_specs=[pl.BlockSpec(memory_space=pltpu.VMEM)] * len(outs),
        scratch_shapes=scratch,
        compiler_params=pltpu.CompilerParams(vmem_limit_bytes=16 * 1024 * 1024),
        cost_estimate=pl.CostEstimate(flops=flops, bytes_accessed=moved, transcendentals=0),
    )(*args)


def dot(left, right):
    return jnp.dot(left, right, preferred_element_type=F32)


def dot_nt(left, right):
    return lax.dot_general(left, right, (((1,), (1,)), ((), ())), preferred_element_type=F32)


def dot_tn(left, right):
    return lax.dot_general(left, right, (((0,), (0,)), ((), ())), preferred_element_type=F32)


def indicator(shape, test):
    row = lax.broadcasted_iota(jnp.int32, shape, 0)
    col = lax.broadcasted_iota(jnp.int32, shape, 1)
    return jnp.where(test(row, col), 1.0, 0.0).astype(BF16)


def splitter():
    def test(row, col):
        part, at = col // BREADTH, col % BREADTH
        return row == 2 * at + part - 1

    return indicator((2 * BREADTH, 4 * BREADTH), test)


def shifter():
    def test(row, col):
        part, at = col // BREADTH, col % BREADTH
        return row == at + 2 * part - 1

    return indicator((BREADTH, 2 * BREADTH), test)


def joiner():
    def test(row, col):
        return col == 2 * (row % BREADTH) + row // BREADTH

    return indicator((2 * BREADTH, 2 * BREADTH), test)


def weights_two(out, turned, flip):
    outs, ins = (16, 32) if flip else (32, 16)
    per = BREADTH // ins
    total = []
    for part in range(64 // per):
        summed = jnp.zeros((outs, BREADTH), F32)
        for at in range(per):
            place = part * per + at
            b, e, a = place // 16, (place // 4) % 4, place % 4
            if max(a, b, e) > 2:
                continue
            if flip:
                a, b, e = 2 - a, 2 - b, 2 - e
            spread = indicator((ins, BREADTH), lambda row, col: col == row + at * ins)
            tap = turned[a * 9 + b * 3 + e]
            summed = summed + (dot(tap, spread) if flip else dot_tn(tap, spread))
        total.append(summed)
    base = jnp.concatenate(total, axis=1)
    for phase in range(8):
        deep, high, wide = phase // 4, (phase // 2) % 2, phase % 2
        move = (high * 16 + wide * 4 + deep) * ins
        full = pltpu.roll(base, move, 1) if move else base
        at = (wide * 4 + deep * 2 + high if flip else phase) * outs
        out[at : at + outs, :] = full.astype(BF16)


def weights_ahead(turned, out):
    weights_two(out, turned, False)


def inside(at, rows):
    return jnp.logical_and(at >= 0, at < rows * axis_count(GROUP))


def edges(own, top, bottom, near, far):
    core = lax.axis_index("core")
    at = 0
    for ref in (top, own, bottom):
        for row in range(ref.shape[0]):
            near[at] = ref[row, 1 - core]
            far[at] = ref[row, core]
            at += 1


def in_order(near, far):
    lower = lax.axis_index("core") == 0

    def below(*at):
        return lax.select(lower, far[at], near[at])

    def above(*at):
        return lax.select(lower, near[at], far[at])

    return below, above


def forward_two(own, near, far, top, bottom, weight, pooled, slope, parts, split):
    split[...] = splitter()
    first = pooled.shape[0] - 6
    first = first * group_index() - 3
    edge = top.shape[0]
    height = own.shape[0]
    below, above = in_order(near, far)

    def place(row, many, block):
        cells = dot(block, split[...]).astype(BF16).reshape(many, 64, 4 * BREADTH)
        for part in range(4):
            to = part * 64
            parts[row : row + many, to : to + 64, :] = cells[:, :, part * BREADTH : (part + 1) * BREADTH]

    for ref, to in ((top, 0), (own, edge), (bottom, edge + height)):
        for row in range(0, ref.shape[0], 4):
            block = []
            for at in range(row, min(row + 4, ref.shape[0])):
                block += [below(to + at), ref[at, 0], ref[at, 1], above(to + at)]
            place(to + row, len(block) // 4, jnp.concatenate(block, axis=0))

    rows = pooled.shape[0]
    for row in range(0, rows, 2):
        cells = [parts[2 * at : 2 * at + 4].reshape(1024, BREADTH) for at in (row, row + 1)]
        pre = dot(weight[...], jnp.concatenate(cells, axis=1))
        small = jnp.exp(-jnp.abs(pre))
        whole = 1.0 + small
        value = 0.3 * pre + 0.7 * (jnp.maximum(pre, 0.0) + jnp.log(whole))
        summed = jnp.sum(value.reshape(8, 32, 2 * BREADTH), axis=0) * 0.125
        for off in range(2):
            half = summed[:, off * BREADTH : (off + 1) * BREADTH]
            kept = inside(first + row + off, rows - 6)
            pooled[row + off] = jnp.where(kept, half, 0.0).astype(BF16)
        if 2 <= row < rows - 2:
            rate = 0.3 + 0.7 * (jnp.where(pre >= 0.0, 1.0, small) / whole)
            slope[row - 2] = rate[:, :BREADTH]
            slope[row - 1] = rate[:, BREADTH:]


def place_shifted(planes, rows, parts, shift, chans):
    span = len(planes) * chans
    step = 256 // chans
    for plane, taken in enumerate(planes):
        at = plane * chans
        for row in range(0, rows, step):
            many = min(step, rows - row)
            block = taken(slice(row, row + many))
            moved = dot(block.reshape(many * chans, BREADTH), shift[...]).astype(BF16)
            moved = moved.reshape(many, chans, 2 * BREADTH)
            parts[row : row + many, at : at + chans, :] = moved[:, :, :BREADTH]
            parts[row : row + many, span + at : span + at + chans, :] = block
            parts[row : row + many, 2 * span + at : 2 * span + at + chans, :] = moved[:, :, BREADTH:]


def side_by_side(parts, row, many, taken, step=1):
    size = taken * parts.shape[1]
    return jnp.concatenate(
        [parts[at * step : at * step + taken].reshape(size, BREADTH) for at in range(row, row + many)],
        axis=1,
    )


def pack(cot, taps, out):
    count, share, width = out.shape
    rows = cot.shape[0] // count
    extra = (width - 896) // BREADTH - rows
    blocks = []
    for part in range(7):
        piece = []
        for tap in range(part * 4, part * 4 + 4):
            at = (tap % 3) * 9 + (tap // 9) * 3 + (tap // 3) % 3
            piece.append(taps[at].astype(F32) if tap < 27 else jnp.zeros((share, 32), F32))
        blocks.append(jnp.concatenate(piece, axis=1).astype(BF16))
    for to in range(count):
        for row in range(rows + extra):
            at = rows * to - extra // 2 + row
            lane = row * BREADTH
            if 0 <= at < cot.shape[0]:
                out[to, :, lane : lane + BREADTH] = cot[at]
            else:
                out[to, :, lane : lane + BREADTH] = jnp.zeros((share, BREADTH), BF16)
        for part in range(7):
            lane = (rows + extra + part) * BREADTH
            out[to, :, lane : lane + BREADTH] = blocks[part]


def middle_three(near, own, far, arrived, grads, parts, to_near, same, to_far, shift, around, turned):
    shift[...] = shifter()
    below, above = in_order(near, far)
    place_shifted((below, own.__getitem__, above), own.shape[0], parts, shift, 32)
    rows = grads.shape[0]
    lower = lax.axis_index("core") == 0
    span = rows * BREADTH
    weight = arrived[:, span:]
    for row in range(0, rows, 4):
        pre = dot(weight[:, :864], side_by_side(parts, row, 4, 3))
        small = jnp.exp(-jnp.abs(pre))
        rate = 0.3 + 0.7 * (jnp.where(pre >= 0.0, 1.0, small) / (1.0 + small))
        full = arrived[:, row * BREADTH : (row + 4) * BREADTH].astype(F32) * rate
        for off in range(4):
            grads[row + off] = full[:, off * BREADTH : (off + 1) * BREADTH].astype(BF16)
    weight = weight.astype(F32)
    flat = jnp.transpose(jnp.concatenate([weight, weight], axis=0))
    lane = lax.broadcasted_iota(jnp.int32, (32, BREADTH), 1)
    for plane in range(3):

        def tap(at, plane=plane):
            first = ((8 - at) * 3 + 2 - plane) * 32
            return flat[first : first + 32]

        to = plane * 32
        for at in range(0, 8, 2):
            pair = jnp.where(lane < 64, tap(at), tap(at + 1))
            turned[to : to + 32, at * 64 : at * 64 + 128] = pair.astype(BF16)
        turned[to : to + 32, 512:576] = tap(8)[:, :64].astype(BF16)
    place_shifted((grads.__getitem__,), rows, around, shift, 64)
    for row in range(0, rows - 2, 2):
        pool = dot(turned[...], side_by_side(around, row, 2, 3))
        for off in range(2):
            half = pool[:, off * BREADTH : (off + 1) * BREADTH]
            up, down = half[:32], half[64:]
            same[row + off] = half[32:64]
            to_near[row + off] = lax.select(lower, up, down).astype(BF16)
            to_far[row + off] = lax.select(lower, down, up).astype(BF16)


def filters_three(grads, parts, out):
    rows = grads.shape[0]
    left = jnp.concatenate([grads[row] for row in range(2, rows - 2)], axis=1)
    full = dot_nt(left, side_by_side(parts, 2, rows - 4, 3))
    out[:, :864] = full
    out[:, 864:] = jnp.zeros((full.shape[0], 160), F32)


def middle_two(near, own, far, slope, parts, three, low, high, lines):
    rows = own.shape[0] - 2
    first = rows * group_index() - 1
    left = []
    for row in range(rows + 2):
        pool = own[row] + near[row].astype(F32) + far[row].astype(F32)
        pool = jnp.where(inside(first + row, rows), pool, 0.0) * 0.125
        full = pool[None] * slope[row].reshape(8, 32, BREADTH)
        full = full.astype(BF16).reshape(256, BREADTH)
        low[row] = full[:128]
        high[row] = full[128:]
        if 1 <= row <= rows:
            left.append(full)
    left = jnp.concatenate(left, axis=1)
    blocks = []
    for off in range(4):
        right = jnp.concatenate([parts[2 * row + 4 + off] for row in range(1, rows + 1)], axis=1)
        blocks.append(dot_nt(left, right))
    total = jnp.zeros((32, 768), F32)
    for phase in range(8):
        deep, tall, wide = phase // 4, (phase // 2) % 2, phase % 2
        part = jnp.concatenate(
            [block[phase * 32 : phase * 32 + 32] for block in blocks[tall : tall + 3]], axis=1
        )
        move = (wide * 4 + deep) * 16
        if move:
            part = pltpu.roll(part, 768 - move, 1)
        total = total + part
    slot = lax.broadcasted_iota(jnp.int32, (32, BREADTH), 1) // 16
    dense = []
    rest = jnp.zeros((32, BREADTH), F32)
    for off in range(3):
        one = total[:, off * 256 : off * 256 + 128]
        two = total[:, off * 256 + 128 : off * 256 + 256]
        one = jnp.where(slot == 3, pltpu.roll(two, 48, 1), one)
        dense.append(jnp.where(slot == 7, pltpu.roll(two, 96, 1), one))
        moved = pltpu.roll(two, 96 + off * 16, 1) if off != 2 else two
        rest = jnp.where(slot == off, moved, rest)
    dense.append(rest)
    for to in range(32):
        quarter, group = to // 8, to % 8
        for part in range(2):
            lane = (quarter * 2 + part) * BREADTH
            block = three[group * 8 : group * 8 + 8, lane : lane + BREADTH]
            lines[to, part * 8 : part * 8 + 8, :] = block
        for block in range(4):
            lines[to, 16 + block : 17 + block, :] = dense[block][to : to + 1]


def slot_of(b, e, a):
    if e < 2:
        return b, e * 4 + a
    return ((b, 3), (b, 7), (3, b))[a]


def backward_two(below, low, high, above, turned, out, parts, shift, join, weight):
    weights_two(weight, turned, True)
    shift[...] = shifter()
    join[...] = joiner()
    for row in range(low.shape[0]):
        block = jnp.concatenate([below[row], low[row], high[row], above[row]], axis=0)
        moved = dot(block, shift[...]).astype(BF16)
        for tall in range(2):
            for deep in range(4):
                at = deep * 128 + tall * 64
                to = deep * 32
                both = 2 * row + tall
                parts[both, to : to + 32, :] = moved[at + 32 : at + 64, :BREADTH]
                parts[both, 128 + to : 160 + to, :] = block[at : at + 32]
                parts[both, 256 + to : 288 + to, :] = block[at + 32 : at + 64]
                parts[both, 384 + to : 416 + to, :] = moved[at : at + 32, BREADTH:]
    for row in range(0, out.shape[0], 2):
        cells = [parts[2 * at + 1 : 2 * at + 5].reshape(2048, BREADTH) for at in (row, row + 1)]
        cells = dot(weight[...], jnp.concatenate(cells, axis=1)).astype(BF16)
        both = [
            jnp.concatenate([cells[:64, at : at + BREADTH], cells[64:, at : at + BREADTH]], axis=1)
            for at in (0, BREADTH)
        ]
        joined = dot(jnp.concatenate(both, axis=0), join[...]).astype(BF16)
        out[row] = joined[:64]
        out[row + 1] = joined[64:]


def spread_out(scale_two, scale_three, lines, two, three):
    for block in range(4):
        rows = [lines[at, 16 + block : 17 + block, :].astype(F32) for at in range(32)]
        flat = jnp.transpose(jnp.concatenate(rows * 4, axis=0) * scale_two)
        for tap in range(27):
            a, b, e = tap // 9, (tap // 3) % 3, tap % 3
            where, slot = slot_of(b, e, a)
            if where == block:
                two[tap] = flat[slot * 16 : slot * 16 + 16, :32]
    for part in range(7):
        at = (part // 2) * 8 + group_index()
        block = lines[at, (part % 2) * 8 : (part % 2) * 8 + 8, :].astype(F32) * scale_three
        for at in range(4):
            tap = part * 4 + at
            if tap < 27:
                b, e, a = tap // 9, (tap // 3) % 3, tap % 3
                three[a * 9 + b * 3 + e] = block[:, at * 32 : at * 32 + 32]


def shifted(axis, step):
    count = axis_count(axis)
    return [(i, i + step) for i in range(count) if 0 <= i + step < count]


def neighbours(first, last, axis):
    return (
        lax.ppermute(last, axis, shifted(axis, 1)),
        lax.ppermute(first, axis, shifted(axis, -1)),
    )


def paired(near, far):
    count = axis_count(DEPTH)
    across = [(i, i + 1) for i in range(1, count - 1, 2)]
    across += [(i + 1, i) for i in range(1, count - 1, 2)]
    return (
        lax.ppermute(near, DEPTH, [(i, i ^ 1) for i in range(count)]),
        lax.ppermute(far, DEPTH, across),
    )


def exchange(blocks, axis):
    return lax.all_to_all(blocks, axis, 0, 0, tiled=True)


def total_of(blocks):
    return jnp.sum(blocks.astype(F32), axis=0).astype(BF16)


def copied(block, names):
    return jnp.broadcast_to(block[None], (axis_count(names),) + block.shape)


def on_device(inputs, weight_two, weight_three, cotangent):
    groups = axis_count(GROUP)
    slabs = axis_count(DEPTH)
    chans, planes, height, breadth = inputs.shape
    cells = planes * slabs * height * groups * breadth
    pool_rows = height // 2
    share = weight_three.shape[3]
    filters = share * groups

    own = jnp.transpose(inputs, (2, 1, 0, 3))
    own, cotangent = lax.optimization_barrier((own, cotangent))
    top, bottom = neighbours(own[:7], own[height - 7 :], GROUP)

    (packed,) = call(
        pack,
        [jax.ShapeDtypeStruct((groups, share, (pool_rows + 4) * BREADTH + 896), BF16)],
        [],
        (jnp.transpose(cotangent[:, 0], (1, 0, 2)), weight_three.reshape(27, share, 32)),
        2 * 64 * 1024,
    )
    packed, bottom = lax.optimization_barrier((packed, bottom))
    arrived = exchange(packed, GROUP).reshape(filters, -1)

    plane = jax.ShapeDtypeStruct((height + 14, chans, breadth), BF16)
    near, far = paired(*call(edges, [plane, plane], [], (own, top, bottom), 1024 * 1024))

    turned = jnp.transpose(weight_two.reshape(27, 32, 16), (0, 2, 1))
    (ahead,) = call(
        weights_ahead,
        [jax.ShapeDtypeStruct((256, 1024), BF16)],
        [],
        (turned,),
        2 * 256 * 1024 * 128,
    )
    ahead, arrived = lax.optimization_barrier((ahead, arrived))

    pooled, slope, parts_two = call(
        forward_two,
        [
            jax.ShapeDtypeStruct((pool_rows + 6, 32, BREADTH), BF16),
            jax.ShapeDtypeStruct((pool_rows + 2, 256, BREADTH), F32),
            jax.ShapeDtypeStruct((height + 14, 256, BREADTH), BF16),
        ],
        [pltpu.VMEM((2 * BREADTH, 4 * BREADTH), BF16)],
        (own, near, far, top, bottom, ahead),
        2 * 14 * 256 * 1024 * 128,
    )

    pool_near, pool_far = paired(pooled, pooled)
    shift = pltpu.VMEM((BREADTH, 2 * BREADTH), BF16)
    terms = jax.ShapeDtypeStruct((pool_rows + 2, 32, BREADTH), BF16)
    grads, parts_three, to_near, same, to_far = call(
        middle_three,
        [
            jax.ShapeDtypeStruct((pool_rows + 4, filters, BREADTH), BF16),
            jax.ShapeDtypeStruct((pool_rows + 6, 288, BREADTH), BF16),
            terms,
            jax.ShapeDtypeStruct(terms.shape, F32),
            terms,
        ],
        [
            shift,
            pltpu.VMEM((pool_rows + 4, 3 * filters, BREADTH), BF16),
            pltpu.VMEM((96, 9 * filters), BF16),
        ],
        (pool_near, pooled, pool_far, arrived),
        2 * 12 * 64 * 864 * 128 * 2,
    )

    terms_near, terms_far = paired(to_near, to_far)
    (local_three,) = call(
        filters_three,
        [jax.ShapeDtypeStruct((filters, 1024), F32)],
        [],
        (grads, parts_three),
        2 * 8 * 64 * 864 * 128,
    )
    plane = jax.ShapeDtypeStruct((pool_rows + 2, 128, BREADTH), BF16)
    low, high, lines = call(
        middle_two,
        [plane, plane, jax.ShapeDtypeStruct((32, 20, BREADTH), F32)],
        [],
        (terms_near, same, terms_far, slope, parts_two, local_three),
        2 * 8 * 256 * 1024 * 128,
    )

    two_below, two_above = neighbours(low, high, DEPTH)
    lines = lines.astype(BF16).reshape(32, 5, 4, BREADTH)
    lines = total_of(exchange(lines, NEAR))
    lines = total_of(exchange(copied(lines, ("z",)), "z"))
    lines = exchange(copied(lines, NEAR), NEAR).reshape(32, 20, BREADTH)
    two, three = call(
        functools.partial(spread_out, 1.0 / math.sqrt(cells), 1.0 / math.sqrt(cells / 8)),
        [
            jax.ShapeDtypeStruct((27, 16, 32), F32),
            jax.ShapeDtypeStruct((27, share, 32), F32),
        ],
        [],
        (lines.astype(F32),),
        2 * 64 * 1024,
    )

    (cells_back,) = call(
        backward_two,
        [jax.ShapeDtypeStruct((pool_rows, 64, 2 * BREADTH), BF16)],
        [
            pltpu.VMEM((height + 4, 512, BREADTH), BF16),
            shift,
            pltpu.VMEM((2 * BREADTH, 2 * BREADTH), BF16),
            pltpu.VMEM((128, 2048), BF16),
        ],
        (two_below, low, high, two_above, turned),
        2 * 8 * 128 * 2048 * 128,
    )
    input_grad = jnp.transpose(
        cells_back.reshape(pool_rows, 2, 2, chans, breadth), (3, 1, 0, 2, 4)
    ).reshape(inputs.shape)
    weight_grad_two = jnp.transpose(two, (0, 2, 1)).reshape(weight_two.shape)
    return (input_grad, weight_grad_two, three.reshape(weight_three.shape))


def solution(mesh):
    parts = jax.sharding.Mesh(mesh.devices.reshape(2, 16, 2, 2, 4), DEPTH + GROUP)
    placed = (
        P(None, DEPTH, GROUP, None),
        P(),
        P(None, None, None, GROUP, None),
        P(GROUP, DEPTH, None, None),
    )
    return jax.shard_map(
        on_device,
        mesh=parts,
        in_specs=placed,
        out_specs=(P(None, DEPTH, GROUP, None), P(), P(None, None, None, GROUP, None)),
        check_vma=False,
    )
```

```python
import functools
import math

import jax
import jax.numpy as jnp
from jax import lax
from jax.experimental import pallas as pl
from jax.experimental.pallas import tpu as pltpu
from jax.sharding import PartitionSpec as P


F32 = jnp.float32
BF16 = jnp.bfloat16
BREADTH = 128
DEPTH = ("yl", "z", "core")
GROUP = ("yh", "x")
NEAR = ("yl", "core", "yh", "x")


def axis_count(names):
    return math.prod(lax.axis_size(name) for name in names)


def group_index():
    return lax.axis_index("yh") * lax.axis_size("x") + lax.axis_index("x")


def call(kernel, outs, scratch, args, flops):
    specs = [pl.BlockSpec(memory_space=pltpu.VMEM)] * len(args)
    moved = sum(math.prod(a.shape) * a.dtype.itemsize for a in list(args) + list(outs))
    return pl.pallas_call(
        kernel,
        out_shape=outs,
        in_specs=specs,
        out_specs=[pl.BlockSpec(memory_space=pltpu.VMEM)] * len(outs),
        scratch_shapes=scratch,
        compiler_params=pltpu.CompilerParams(vmem_limit_bytes=16 * 1024 * 1024),
        cost_estimate=pl.CostEstimate(flops=flops, bytes_accessed=moved, transcendentals=0),
    )(*args)


def dot(left, right):
    return jnp.dot(left, right, preferred_element_type=F32)


def dot_nt(left, right):
    return lax.dot_general(left, right, (((1,), (1,)), ((), ())), preferred_element_type=F32)


def dot_tn(left, right):
    return lax.dot_general(left, right, (((0,), (0,)), ((), ())), preferred_element_type=F32)


def indicator(shape, test):
    row = lax.broadcasted_iota(jnp.int32, shape, 0)
    col = lax.broadcasted_iota(jnp.int32, shape, 1)
    return jnp.where(test(row, col), 1.0, 0.0).astype(BF16)


def splitter():
    def test(row, col):
        part, at = col // BREADTH, col % BREADTH
        return row == 2 * at + part - 1

    return indicator((2 * BREADTH, 4 * BREADTH), test)


def shifter():
    def test(row, col):
        part, at = col // BREADTH, col % BREADTH
        return row == at + 2 * part - 1

    return indicator((BREADTH, 2 * BREADTH), test)


def joiner():
    def test(row, col):
        return col == 2 * (row % BREADTH) + row // BREADTH

    return indicator((2 * BREADTH, 2 * BREADTH), test)


def weights_two(out, turned, flip):
    outs, ins = (16, 32) if flip else (32, 16)
    per = BREADTH // ins
    total = []
    for part in range(64 // per):
        summed = jnp.zeros((outs, BREADTH), F32)
        for at in range(per):
            place = part * per + at
            b, e, a = place // 16, (place // 4) % 4, place % 4
            if max(a, b, e) > 2:
                continue
            if flip:
                a, b, e = 2 - a, 2 - b, 2 - e
            spread = indicator((ins, BREADTH), lambda row, col: col == row + at * ins)
            tap = turned[a * 9 + b * 3 + e]
            summed = summed + (dot(tap, spread) if flip else dot_tn(tap, spread))
        total.append(summed)
    base = jnp.concatenate(total, axis=1)
    for phase in range(8):
        deep, high, wide = phase // 4, (phase // 2) % 2, phase % 2
        move = (high * 16 + wide * 4 + deep) * ins
        full = pltpu.roll(base, move, 1) if move else base
        at = (wide * 4 + deep * 2 + high if flip else phase) * outs
        out[at : at + outs, :] = full.astype(BF16)


def weights_ahead(turned, out):
    weights_two(out, turned, False)


def inside(at, rows):
    return jnp.logical_and(at >= 0, at < rows * axis_count(GROUP))


def sides(own, near, far):
    odd = lax.rem(lax.axis_index("x"), 2)
    rest = own.shape[0] - near.shape[0]
    for row in range(near.shape[0]):
        near[row] = own[row + rest * (1 - odd)]
        far[row] = own[row + rest * odd]


def edges(own, near_rows, far_rows, near, far):
    core = lax.axis_index("core")
    top, bottom = in_order(near_rows, far_rows, "x")
    count, height = near_rows.shape[0], own.shape[0]
    for row in range(count):
        near[row] = top(row, 1 - core)
        far[row] = top(row, core)
        near[count + height + row] = bottom(row, 1 - core)
        far[count + height + row] = bottom(row, core)
    for row in range(height):
        near[count + row] = own[row, 1 - core]
        far[count + row] = own[row, core]


def in_order(near, far, name="core"):
    lower = lax.rem(lax.axis_index(name), 2) == 0

    def below(*at):
        return lax.select(lower, far[at], near[at])

    def above(*at):
        return lax.select(lower, near[at], far[at])

    return below, above


def forward_two(own, near, far, near_rows, far_rows, weight, pooled, slope, parts, split):
    split[...] = splitter()
    first = pooled.shape[0] - 6
    first = first * group_index() - 3
    edge = near_rows.shape[0]
    height = own.shape[0]
    below, above = in_order(near, far)
    top, bottom = in_order(near_rows, far_rows, "x")

    def place(row, many, block):
        cells = dot(block, split[...]).astype(BF16).reshape(many, 64, 4 * BREADTH)
        for part in range(4):
            to = part * 64
            parts[row : row + many, to : to + 64, :] = cells[:, :, part * BREADTH : (part + 1) * BREADTH]

    for taken, to, many in ((top, 0, edge), (own, edge, height), (bottom, edge + height, edge)):
        for row in range(0, many, 4):
            block = []
            for at in range(row, min(row + 4, many)):
                if taken is own:
                    both = [own[at, 0], own[at, 1]]
                else:
                    both = [taken(at, 0), taken(at, 1)]
                block += [below(to + at)] + both + [above(to + at)]
            place(to + row, len(block) // 4, jnp.concatenate(block, axis=0))

    rows = pooled.shape[0]
    for row in range(0, rows, 2):
        cells = [parts[2 * at : 2 * at + 4].reshape(1024, BREADTH) for at in (row, row + 1)]
        pre = dot(weight[...], jnp.concatenate(cells, axis=1))
        small = jnp.exp(-jnp.abs(pre))
        whole = 1.0 + small
        value = 0.3 * pre + 0.7 * (jnp.maximum(pre, 0.0) + jnp.log(whole))
        summed = jnp.sum(value.reshape(8, 32, 2 * BREADTH), axis=0) * 0.125
        for off in range(2):
            half = summed[:, off * BREADTH : (off + 1) * BREADTH]
            kept = inside(first + row + off, rows - 6)
            pooled[row + off] = jnp.where(kept, half, 0.0).astype(BF16)
        if 2 <= row < rows - 2:
            rate = 0.3 + 0.7 * (jnp.where(pre >= 0.0, 1.0, small) / whole)
            slope[row - 2] = rate[:, :BREADTH]
            slope[row - 1] = rate[:, BREADTH:]


def place_shifted(planes, rows, parts, shift, chans):
    span = len(planes) * chans
    step = 256 // chans
    for plane, taken in enumerate(planes):
        at = plane * chans
        for row in range(0, rows, step):
            many = min(step, rows - row)
            block = taken(slice(row, row + many))
            moved = dot(block.reshape(many * chans, BREADTH), shift[...]).astype(BF16)
            moved = moved.reshape(many, chans, 2 * BREADTH)
            parts[row : row + many, at : at + chans, :] = moved[:, :, :BREADTH]
            parts[row : row + many, span + at : span + at + chans, :] = block
            parts[row : row + many, 2 * span + at : 2 * span + at + chans, :] = moved[:, :, BREADTH:]


def side_by_side(parts, row, many, taken, step=1):
    size = taken * parts.shape[1]
    return jnp.concatenate(
        [parts[at * step : at * step + taken].reshape(size, BREADTH) for at in range(row, row + many)],
        axis=1,
    )


def pack(cot, taps, out):
    count, share, width = out.shape
    rows = cot.shape[0] // count
    extra = (width - 896) // BREADTH - rows
    blocks = []
    for part in range(7):
        piece = []
        for tap in range(part * 4, part * 4 + 4):
            at = (tap % 3) * 9 + (tap // 9) * 3 + (tap // 3) % 3
            piece.append(taps[at].astype(F32) if tap < 27 else jnp.zeros((share, 32), F32))
        blocks.append(jnp.concatenate(piece, axis=1).astype(BF16))
    for to in range(count):
        for row in range(rows + extra):
            at = rows * to - extra // 2 + row
            lane = row * BREADTH
            if 0 <= at < cot.shape[0]:
                out[to, :, lane : lane + BREADTH] = cot[at]
            else:
                out[to, :, lane : lane + BREADTH] = jnp.zeros((share, BREADTH), BF16)
        for part in range(7):
            lane = (rows + extra + part) * BREADTH
            out[to, :, lane : lane + BREADTH] = blocks[part]


def middle_three(near, own, far, arrived, grads, parts, to_near, same, to_far, shift, around, turned):
    shift[...] = shifter()
    below, above = in_order(near, far)
    place_shifted((below, own.__getitem__, above), own.shape[0], parts, shift, 32)
    rows = grads.shape[0]
    lower = lax.axis_index("core") == 0
    span = rows * BREADTH
    weight = arrived[:, span:]
    for row in range(0, rows, 4):
        pre = dot(weight[:, :864], side_by_side(parts, row, 4, 3))
        small = jnp.exp(-jnp.abs(pre))
        rate = 0.3 + 0.7 * (jnp.where(pre >= 0.0, 1.0, small) / (1.0 + small))
        full = arrived[:, row * BREADTH : (row + 4) * BREADTH].astype(F32) * rate
        for off in range(4):
            grads[row + off] = full[:, off * BREADTH : (off + 1) * BREADTH].astype(BF16)
    weight = weight.astype(F32)
    flat = jnp.transpose(jnp.concatenate([weight, weight], axis=0))
    lane = lax.broadcasted_iota(jnp.int32, (32, BREADTH), 1)
    for plane in range(3):

        def tap(at, plane=plane):
            first = ((8 - at) * 3 + 2 - plane) * 32
            return flat[first : first + 32]

        to = plane * 32
        for at in range(0, 8, 2):
            pair = jnp.where(lane < 64, tap(at), tap(at + 1))
            turned[to : to + 32, at * 64 : at * 64 + 128] = pair.astype(BF16)
        turned[to : to + 32, 512:576] = tap(8)[:, :64].astype(BF16)
    place_shifted((grads.__getitem__,), rows, around, shift, 64)
    for row in range(0, rows - 2, 2):
        pool = dot(turned[...], side_by_side(around, row, 2, 3))
        for off in range(2):
            half = pool[:, off * BREADTH : (off + 1) * BREADTH]
            up, down = half[:32], half[64:]
            same[row + off] = half[32:64]
            to_near[row + off] = lax.select(lower, up, down).astype(BF16)
            to_far[row + off] = lax.select(lower, down, up).astype(BF16)


def filters_three(grads, parts, out):
    rows = grads.shape[0]
    left = jnp.concatenate([grads[row] for row in range(2, rows - 2)], axis=1)
    full = dot_nt(left, side_by_side(parts, 2, rows - 4, 3))
    out[:, :864] = full
    out[:, 864:] = jnp.zeros((full.shape[0], 160), F32)


def middle_two(near, own, far, slope, parts, three, low, high, lines):
    rows = own.shape[0] - 2
    first = rows * group_index() - 1
    left = []
    for row in range(rows + 2):
        pool = own[row] + near[row].astype(F32) + far[row].astype(F32)
        pool = jnp.where(inside(first + row, rows), pool, 0.0) * 0.125
        full = pool[None] * slope[row].reshape(8, 32, BREADTH)
        full = full.astype(BF16).reshape(256, BREADTH)
        low[row] = full[:128]
        high[row] = full[128:]
        if 1 <= row <= rows:
            left.append(full)
    left = jnp.concatenate(left, axis=1)
    blocks = []
    for off in range(4):
        right = jnp.concatenate([parts[2 * row + 4 + off] for row in range(1, rows + 1)], axis=1)
        blocks.append(dot_nt(left, right))
    total = jnp.zeros((32, 768), F32)
    for phase in range(8):
        deep, tall, wide = phase // 4, (phase // 2) % 2, phase % 2
        part = jnp.concatenate(
            [block[phase * 32 : phase * 32 + 32] for block in blocks[tall : tall + 3]], axis=1
        )
        move = (wide * 4 + deep) * 16
        if move:
            part = pltpu.roll(part, 768 - move, 1)
        total = total + part
    slot = lax.broadcasted_iota(jnp.int32, (32, BREADTH), 1) // 16
    dense = []
    rest = jnp.zeros((32, BREADTH), F32)
    for off in range(3):
        one = total[:, off * 256 : off * 256 + 128]
        two = total[:, off * 256 + 128 : off * 256 + 256]
        one = jnp.where(slot == 3, pltpu.roll(two, 48, 1), one)
        dense.append(jnp.where(slot == 7, pltpu.roll(two, 96, 1), one))
        moved = pltpu.roll(two, 96 + off * 16, 1) if off != 2 else two
        rest = jnp.where(slot == off, moved, rest)
    dense.append(rest)
    for to in range(32):
        quarter, group = to // 8, to % 8
        for part in range(2):
            lane = (quarter * 2 + part) * BREADTH
            block = three[group * 8 : group * 8 + 8, lane : lane + BREADTH]
            lines[to, part * 8 : part * 8 + 8, :] = block
        for block in range(4):
            lines[to, 16 + block : 17 + block, :] = dense[block][to : to + 1]


def slot_of(b, e, a):
    if e < 2:
        return b, e * 4 + a
    return ((b, 3), (b, 7), (3, b))[a]


def backward_two(below, low, high, above, turned, out, parts, shift, join, weight):
    weights_two(weight, turned, True)
    shift[...] = shifter()
    join[...] = joiner()
    for row in range(low.shape[0]):
        block = jnp.concatenate([below[row], low[row], high[row], above[row]], axis=0)
        moved = dot(block, shift[...]).astype(BF16)
        for tall in range(2):
            for deep in range(4):
                at = deep * 128 + tall * 64
                to = deep * 32
                both = 2 * row + tall
                parts[both, to : to + 32, :] = moved[at + 32 : at + 64, :BREADTH]
                parts[both, 128 + to : 160 + to, :] = block[at : at + 32]
                parts[both, 256 + to : 288 + to, :] = block[at + 32 : at + 64]
                parts[both, 384 + to : 416 + to, :] = moved[at : at + 32, BREADTH:]
    for row in range(0, out.shape[0], 2):
        cells = [parts[2 * at + 1 : 2 * at + 5].reshape(2048, BREADTH) for at in (row, row + 1)]
        cells = dot(weight[...], jnp.concatenate(cells, axis=1)).astype(BF16)
        both = [
            jnp.concatenate([cells[:64, at : at + BREADTH], cells[64:, at : at + BREADTH]], axis=1)
            for at in (0, BREADTH)
        ]
        joined = dot(jnp.concatenate(both, axis=0), join[...]).astype(BF16)
        out[row] = joined[:64]
        out[row + 1] = joined[64:]


def spread_out(scale_two, scale_three, lines, two, three):
    for block in range(4):
        rows = [lines[at, 4].astype(F32)[block : block + 1] for at in range(32)]
        flat = jnp.transpose(jnp.concatenate(rows * 4, axis=0) * scale_two)
        for tap in range(27):
            a, b, e = tap // 9, (tap // 3) % 3, tap % 3
            where, slot = slot_of(b, e, a)
            if where == block:
                two[tap] = flat[slot * 16 : slot * 16 + 16, :32]
    for part in range(7):
        at = (part // 2) * 8 + group_index()
        first = (part % 2) * 2
        block = [lines[at, first].astype(F32), lines[at, first + 1].astype(F32)]
        block = jnp.concatenate(block, axis=0) * scale_three
        for at in range(4):
            tap = part * 4 + at
            if tap < 27:
                b, e, a = tap // 9, (tap // 3) % 3, tap % 3
                three[a * 9 + b * 3 + e] = block[:, at * 32 : at * 32 + 32]


def shifted(axis, step):
    count = axis_count(axis)
    return [(i, i + step) for i in range(count) if 0 <= i + step < count]


def neighbours(first, last, axis):
    return (
        lax.ppermute(last, axis, shifted(axis, 1)),
        lax.ppermute(first, axis, shifted(axis, -1)),
    )


def paired(near, far, names=DEPTH):
    count = axis_count(names)
    across = [(i, i + 1) for i in range(1, count - 1, 2)]
    across += [(i + 1, i) for i in range(1, count - 1, 2)]
    return (
        lax.ppermute(near, names, [(i, i ^ 1) for i in range(count)]),
        lax.ppermute(far, names, across),
    )


def exchange(blocks, axis):
    return lax.all_to_all(blocks, axis, 0, 0, tiled=True)


def total_of(blocks):
    return jnp.sum(blocks.astype(F32), axis=0).astype(BF16)


def copied(block, names):
    return jnp.broadcast_to(block[None], (axis_count(names),) + block.shape)


def on_device(inputs, weight_two, weight_three, cotangent):
    groups = axis_count(GROUP)
    slabs = axis_count(DEPTH)
    chans, planes, height, breadth = inputs.shape
    cells = planes * slabs * height * groups * breadth
    pool_rows = height // 2
    share = weight_three.shape[3]
    filters = share * groups

    own = jnp.transpose(inputs, (2, 1, 0, 3))
    own, cotangent = lax.optimization_barrier((own, cotangent))
    rows = jax.ShapeDtypeStruct((7, planes, chans, breadth), BF16)
    near_rows, far_rows = paired(*call(sides, [rows, rows], [], (own,), 1024), GROUP)

    (packed,) = call(
        pack,
        [jax.ShapeDtypeStruct((groups, share, (pool_rows + 4) * BREADTH + 896), BF16)],
        [],
        (jnp.transpose(cotangent[:, 0], (1, 0, 2)), weight_three.reshape(27, share, 32)),
        2 * 64 * 1024,
    )
    packed, near_rows = lax.optimization_barrier((packed, near_rows))
    arrived = exchange(packed, GROUP).reshape(filters, -1)

    plane = jax.ShapeDtypeStruct((height + 14, chans, breadth), BF16)
    near, far = paired(*call(edges, [plane, plane], [], (own, near_rows, far_rows), 1024 * 1024))

    turned = jnp.transpose(weight_two.reshape(27, 32, 16), (0, 2, 1))
    (ahead,) = call(
        weights_ahead,
        [jax.ShapeDtypeStruct((256, 1024), BF16)],
        [],
        (turned,),
        2 * 256 * 1024 * 128,
    )
    ahead, arrived = lax.optimization_barrier((ahead, arrived))

    pooled, slope, parts_two = call(
        forward_two,
        [
            jax.ShapeDtypeStruct((pool_rows + 6, 32, BREADTH), BF16),
            jax.ShapeDtypeStruct((pool_rows + 2, 256, BREADTH), F32),
            jax.ShapeDtypeStruct((height + 14, 256, BREADTH), BF16),
        ],
        [pltpu.VMEM((2 * BREADTH, 4 * BREADTH), BF16)],
        (own, near, far, near_rows, far_rows, ahead),
        2 * 14 * 256 * 1024 * 128,
    )

    pool_near, pool_far = paired(pooled, pooled)
    shift = pltpu.VMEM((BREADTH, 2 * BREADTH), BF16)
    terms = jax.ShapeDtypeStruct((pool_rows + 2, 32, BREADTH), BF16)
    grads, parts_three, to_near, same, to_far = call(
        middle_three,
        [
            jax.ShapeDtypeStruct((pool_rows + 4, filters, BREADTH), BF16),
            jax.ShapeDtypeStruct((pool_rows + 6, 288, BREADTH), BF16),
            terms,
            jax.ShapeDtypeStruct(terms.shape, F32),
            terms,
        ],
        [
            shift,
            pltpu.VMEM((pool_rows + 4, 3 * filters, BREADTH), BF16),
            pltpu.VMEM((96, 9 * filters), BF16),
        ],
        (pool_near, pooled, pool_far, arrived),
        2 * 12 * 64 * 864 * 128 * 2,
    )

    terms_near, terms_far = paired(to_near, to_far)
    (local_three,) = call(
        filters_three,
        [jax.ShapeDtypeStruct((filters, 1024), F32)],
        [],
        (grads, parts_three),
        2 * 8 * 64 * 864 * 128,
    )
    plane = jax.ShapeDtypeStruct((pool_rows + 2, 128, BREADTH), BF16)
    low, high, lines = call(
        middle_two,
        [plane, plane, jax.ShapeDtypeStruct((32, 20, BREADTH), F32)],
        [],
        (terms_near, same, terms_far, slope, parts_two, local_three),
        2 * 8 * 256 * 1024 * 128,
    )

    two_below, two_above = neighbours(low, high, DEPTH)
    lines = lines.astype(BF16).reshape(32, 5, 4, BREADTH)
    lines = total_of(exchange(lines, NEAR))
    lines = total_of(exchange(copied(lines, ("z",)), "z"))
    lines = exchange(copied(lines, NEAR), NEAR)
    two, three = call(
        functools.partial(spread_out, 1.0 / math.sqrt(cells), 1.0 / math.sqrt(cells / 8)),
        [
            jax.ShapeDtypeStruct((27, 16, 32), F32),
            jax.ShapeDtypeStruct((27, share, 32), F32),
        ],
        [],
        (lines,),
        2 * 64 * 1024,
    )

    (cells_back,) = call(
        backward_two,
        [jax.ShapeDtypeStruct((pool_rows, 64, 2 * BREADTH), BF16)],
        [
            pltpu.VMEM((height + 4, 512, BREADTH), BF16),
            shift,
            pltpu.VMEM((2 * BREADTH, 2 * BREADTH), BF16),
            pltpu.VMEM((128, 2048), BF16),
        ],
        (two_below, low, high, two_above, turned),
        2 * 8 * 128 * 2048 * 128,
    )
    input_grad = jnp.transpose(
        cells_back.reshape(pool_rows, 2, 2, chans, breadth), (3, 1, 0, 2, 4)
    ).reshape(inputs.shape)
    weight_grad_two = jnp.transpose(two, (0, 2, 1)).reshape(weight_two.shape)
    return (input_grad, weight_grad_two, three.reshape(weight_three.shape))


def solution(mesh):
    parts = jax.sharding.Mesh(mesh.devices.reshape(2, 16, 2, 2, 4), DEPTH + GROUP)
    placed = (
        P(None, DEPTH, GROUP, None),
        P(),
        P(None, None, None, GROUP, None),
        P(GROUP, DEPTH, None, None),
    )
    return jax.shard_map(
        on_device,
        mesh=parts,
        in_specs=placed,
        out_specs=(P(None, DEPTH, GROUP, None), P(), P(None, None, None, GROUP, None)),
        check_vma=False,
    )
```

```python
import functools
import math

import jax
import jax.numpy as jnp
from jax import lax
from jax.experimental import pallas as pl
from jax.experimental.pallas import tpu as pltpu
from jax.sharding import PartitionSpec as P


F32 = jnp.float32
BF16 = jnp.bfloat16
BREADTH = 128
DEPTH = ("yl", "z", "core")
GROUP = ("yh", "x")
NEAR = ("yl", "core", "yh", "x")


def axis_count(names):
    return math.prod(lax.axis_size(name) for name in names)


def group_index():
    return lax.axis_index("yh") * lax.axis_size("x") + lax.axis_index("x")


def call(kernel, outs, scratch, args, flops, outside=0, room=16):
    specs = [pl.BlockSpec(memory_space=pl.ANY)] * outside
    specs += [pl.BlockSpec(memory_space=pltpu.VMEM)] * (len(args) - outside)
    moved = sum(math.prod(a.shape) * a.dtype.itemsize for a in list(args) + list(outs))
    return pl.pallas_call(
        kernel,
        out_shape=outs,
        in_specs=specs,
        out_specs=[pl.BlockSpec(memory_space=pltpu.VMEM)] * len(outs),
        scratch_shapes=scratch,
        compiler_params=pltpu.CompilerParams(vmem_limit_bytes=room * 1024 * 1024),
        cost_estimate=pl.CostEstimate(flops=flops, bytes_accessed=moved, transcendentals=0),
    )(*args)


def dot(left, right):
    return jnp.dot(left, right, preferred_element_type=F32)


def dot_nt(left, right):
    return lax.dot_general(left, right, (((1,), (1,)), ((), ())), preferred_element_type=F32)


def dot_tn(left, right):
    return lax.dot_general(left, right, (((0,), (0,)), ((), ())), preferred_element_type=F32)


def indicator(shape, test):
    row = lax.broadcasted_iota(jnp.int32, shape, 0)
    col = lax.broadcasted_iota(jnp.int32, shape, 1)
    return jnp.where(test(row, col), 1.0, 0.0).astype(BF16)


def splitter():
    def test(row, col):
        part, at = col // BREADTH, col % BREADTH
        return row == 2 * at + part - 1

    return indicator((2 * BREADTH, 4 * BREADTH), test)


def shifter():
    def test(row, col):
        part, at = col // BREADTH, col % BREADTH
        return row == at + 2 * part - 1

    return indicator((BREADTH, 2 * BREADTH), test)


def joiner():
    def test(row, col):
        return col == 2 * (row % BREADTH) + row // BREADTH

    return indicator((2 * BREADTH, 2 * BREADTH), test)


def weights_two(out, turned, flip):
    outs, ins = (16, 32) if flip else (32, 16)
    per = BREADTH // ins
    total = []
    for part in range(64 // per):
        summed = jnp.zeros((outs, BREADTH), F32)
        for at in range(per):
            place = part * per + at
            b, e, a = place // 16, (place // 4) % 4, place % 4
            if max(a, b, e) > 2:
                continue
            if flip:
                a, b, e = 2 - a, 2 - b, 2 - e
            spread = indicator((ins, BREADTH), lambda row, col: col == row + at * ins)
            tap = turned[a * 9 + b * 3 + e]
            summed = summed + (dot(tap, spread) if flip else dot_tn(tap, spread))
        total.append(summed)
    base = jnp.concatenate(total, axis=1)
    for phase in range(8):
        deep, high, wide = phase // 4, (phase // 2) % 2, phase % 2
        move = (high * 16 + wide * 4 + deep) * ins
        full = pltpu.roll(base, move, 1) if move else base
        at = (wide * 4 + deep * 2 + high if flip else phase) * outs
        out[at : at + outs, :] = full.astype(BF16)


def weights_ahead(turned, out):
    weights_two(out, turned, False)


def inside(at, rows):
    return jnp.logical_and(at >= 0, at < rows * axis_count(GROUP))


def sides(own, near, far):
    odd = lax.rem(lax.axis_index("x"), 2)
    rest = own.shape[0] - near.shape[0]
    for row in range(near.shape[0]):
        near[row] = own[row + rest * (1 - odd)]
        far[row] = own[row + rest * odd]


def edges(own, near_rows, far_rows, near, far):
    core = lax.axis_index("core")
    top, bottom = in_order(near_rows, far_rows, "x")
    count, height = near_rows.shape[0], own.shape[0]
    for row in range(count):
        near[row] = top(row, 1 - core)
        far[row] = top(row, core)
        near[count + height + row] = bottom(row, 1 - core)
        far[count + height + row] = bottom(row, core)
    for row in range(height):
        near[count + row] = own[row, 1 - core]
        far[count + row] = own[row, core]


def in_order(near, far, name="core"):
    lower = lax.rem(lax.axis_index(name), 2) == 0

    def below(*at):
        return lax.select(lower, far[at], near[at])

    def above(*at):
        return lax.select(lower, near[at], far[at])

    return below, above


def forward_two(own, near, far, near_rows, far_rows, weight, pooled, slope, parts, split):
    split[...] = splitter()
    first = pooled.shape[0] - 6
    first = first * group_index() - 3
    edge = near_rows.shape[0]
    height = own.shape[0]
    below, above = in_order(near, far)
    top, bottom = in_order(near_rows, far_rows, "x")

    def place(row, many, block):
        cells = dot(block, split[...]).astype(BF16).reshape(many, 64, 4 * BREADTH)
        for part in range(4):
            to = part * 64
            parts[row : row + many, to : to + 64, :] = cells[:, :, part * BREADTH : (part + 1) * BREADTH]

    for taken, to, many in ((top, 0, edge), (own, edge, height), (bottom, edge + height, edge)):
        for row in range(0, many, 4):
            block = []
            for at in range(row, min(row + 4, many)):
                if taken is own:
                    both = [own[at, 0], own[at, 1]]
                else:
                    both = [taken(at, 0), taken(at, 1)]
                block += [below(to + at)] + both + [above(to + at)]
            place(to + row, len(block) // 4, jnp.concatenate(block, axis=0))

    rows = pooled.shape[0]
    for row in range(0, rows, 2):
        cells = [parts[2 * at : 2 * at + 4].reshape(1024, BREADTH) for at in (row, row + 1)]
        pre = dot(weight[...], jnp.concatenate(cells, axis=1))
        small = jnp.exp(-jnp.abs(pre))
        whole = 1.0 + small
        value = 0.3 * pre + 0.7 * (jnp.maximum(pre, 0.0) + jnp.log(whole))
        summed = jnp.sum(value.reshape(8, 32, 2 * BREADTH), axis=0) * 0.125
        for off in range(2):
            half = summed[:, off * BREADTH : (off + 1) * BREADTH]
            kept = inside(first + row + off, rows - 6)
            pooled[row + off] = jnp.where(kept, half, 0.0).astype(BF16)
        if 2 <= row < rows - 2:
            rate = 0.3 + 0.7 * (jnp.where(pre >= 0.0, 1.0, small) / whole)
            slope[row - 2] = rate[:, :BREADTH]
            slope[row - 1] = rate[:, BREADTH:]


def place_shifted(planes, rows, parts, shift, chans):
    span = len(planes) * chans
    step = 256 // chans
    for plane, taken in enumerate(planes):
        at = plane * chans
        for row in range(0, rows, step):
            many = min(step, rows - row)
            block = taken(slice(row, row + many))
            moved = dot(block.reshape(many * chans, BREADTH), shift[...]).astype(BF16)
            moved = moved.reshape(many, chans, 2 * BREADTH)
            parts[row : row + many, at : at + chans, :] = moved[:, :, :BREADTH]
            parts[row : row + many, span + at : span + at + chans, :] = block
            parts[row : row + many, 2 * span + at : 2 * span + at + chans, :] = moved[:, :, BREADTH:]


def side_by_side(parts, row, many, taken, step=1):
    size = taken * parts.shape[1]
    return jnp.concatenate(
        [parts[at * step : at * step + taken].reshape(size, BREADTH) for at in range(row, row + many)],
        axis=1,
    )


def pack(taps_in, cot_in, out, taps, rows_in, done):
    copies = [
        pltpu.make_async_copy(cot_in, rows_in, done.at[0]),
        pltpu.make_async_copy(taps_in, taps, done.at[1]),
    ]
    for copy in copies:
        copy.start()
    copies[0].wait()
    count, share, width = out.shape
    cot = jnp.swapaxes(rows_in[...].astype(F32), 0, 1).astype(BF16)
    rows = cot.shape[0] // count
    extra = (width - 896) // BREADTH - rows
    for to in range(count):
        for row in range(rows + extra):
            at = rows * to - extra // 2 + row
            lane = row * BREADTH
            if 0 <= at < cot.shape[0]:
                out[to, :, lane : lane + BREADTH] = cot[at]
            else:
                out[to, :, lane : lane + BREADTH] = jnp.zeros((share, BREADTH), BF16)
    copies[1].wait()
    blocks = []
    for part in range(7):
        piece = []
        for tap in range(part * 4, part * 4 + 4):
            at = (tap % 3) * 9 + (tap // 9) * 3 + (tap // 3) % 3
            piece.append(taps[at].astype(F32) if tap < 27 else jnp.zeros((share, 32), F32))
        blocks.append(jnp.concatenate(piece, axis=1).astype(BF16))
    for to in range(count):
        for part in range(7):
            lane = (rows + extra + part) * BREADTH
            out[to, :, lane : lane + BREADTH] = blocks[part]


def middle_three(near, own, far, arrived, grads, parts, to_near, same, to_far, shift, around, turned):
    shift[...] = shifter()
    below, above = in_order(near, far)
    place_shifted((below, own.__getitem__, above), own.shape[0], parts, shift, 32)
    rows = grads.shape[0]
    lower = lax.axis_index("core") == 0
    span = rows * BREADTH
    weight = arrived[:, span:]
    for row in range(0, rows, 4):
        pre = dot(weight[:, :864], side_by_side(parts, row, 4, 3))
        small = jnp.exp(-jnp.abs(pre))
        rate = 0.3 + 0.7 * (jnp.where(pre >= 0.0, 1.0, small) / (1.0 + small))
        full = arrived[:, row * BREADTH : (row + 4) * BREADTH].astype(F32) * rate
        for off in range(4):
            grads[row + off] = full[:, off * BREADTH : (off + 1) * BREADTH].astype(BF16)
    weight = weight.astype(F32)
    flat = jnp.transpose(jnp.concatenate([weight, weight], axis=0))
    lane = lax.broadcasted_iota(jnp.int32, (32, BREADTH), 1)
    for plane in range(3):

        def tap(at, plane=plane):
            first = ((8 - at) * 3 + 2 - plane) * 32
            return flat[first : first + 32]

        to = plane * 32
        for at in range(0, 8, 2):
            pair = jnp.where(lane < 64, tap(at), tap(at + 1))
            turned[to : to + 32, at * 64 : at * 64 + 128] = pair.astype(BF16)
        turned[to : to + 32, 512:576] = tap(8)[:, :64].astype(BF16)
    place_shifted((grads.__getitem__,), rows, around, shift, 64)
    for row in range(0, rows - 2, 2):
        pool = dot(turned[...], side_by_side(around, row, 2, 3))
        for off in range(2):
            half = pool[:, off * BREADTH : (off + 1) * BREADTH]
            up, down = half[:32], half[64:]
            same[row + off] = half[32:64]
            to_near[row + off] = lax.select(lower, up, down).astype(BF16)
            to_far[row + off] = lax.select(lower, down, up).astype(BF16)


def filters_three(grads, parts, out):
    rows = grads.shape[0]
    left = jnp.concatenate([grads[row] for row in range(2, rows - 2)], axis=1)
    full = dot_nt(left, side_by_side(parts, 2, rows - 4, 3))
    out[:, :864] = full
    out[:, 864:] = jnp.zeros((full.shape[0], 160), F32)


def middle_two(near, own, far, slope, parts, three, low, high, lines):
    rows = own.shape[0] - 2
    first = rows * group_index() - 1
    left = []
    for row in range(rows + 2):
        pool = own[row] + near[row].astype(F32) + far[row].astype(F32)
        pool = jnp.where(inside(first + row, rows), pool, 0.0) * 0.125
        full = pool[None] * slope[row].reshape(8, 32, BREADTH)
        full = full.astype(BF16).reshape(256, BREADTH)
        low[row] = full[:128]
        high[row] = full[128:]
        if 1 <= row <= rows:
            left.append(full)
    left = jnp.concatenate(left, axis=1)
    blocks = []
    for off in range(4):
        right = jnp.concatenate([parts[2 * row + 4 + off] for row in range(1, rows + 1)], axis=1)
        blocks.append(dot_nt(left, right))
    total = jnp.zeros((32, 768), F32)
    for phase in range(8):
        deep, tall, wide = phase // 4, (phase // 2) % 2, phase % 2
        part = jnp.concatenate(
            [block[phase * 32 : phase * 32 + 32] for block in blocks[tall : tall + 3]], axis=1
        )
        move = (wide * 4 + deep) * 16
        if move:
            part = pltpu.roll(part, 768 - move, 1)
        total = total + part
    slot = lax.broadcasted_iota(jnp.int32, (32, BREADTH), 1) // 16
    dense = []
    rest = jnp.zeros((32, BREADTH), F32)
    for off in range(3):
        one = total[:, off * 256 : off * 256 + 128]
        two = total[:, off * 256 + 128 : off * 256 + 256]
        one = jnp.where(slot == 3, pltpu.roll(two, 48, 1), one)
        dense.append(jnp.where(slot == 7, pltpu.roll(two, 96, 1), one))
        moved = pltpu.roll(two, 96 + off * 16, 1) if off != 2 else two
        rest = jnp.where(slot == off, moved, rest)
    dense.append(rest)
    for to in range(32):
        quarter, group = to // 8, to % 8
        row = 0
        while row < 14:
            part, off = divmod(quarter * 14 + row, 8)
            many = min(8 - off, 14 - row)
            at, lane = group * 8 + off, part * BREADTH
            lines[to, row : row + many, :] = three[at : at + many, lane : lane + BREADTH]
            row += many
        for block in range(4):
            lines[to, 14 + block : 15 + block, :] = dense[block][to : to + 1]


def slot_of(b, e, a):
    if e < 2:
        return b, e * 4 + a
    return ((b, 3), (b, 7), (3, b))[a]


def backward_two(below, low, high, above, turned, out, parts, shift, join, weight):
    weights_two(weight, turned, True)
    shift[...] = shifter()
    join[...] = joiner()
    for row in range(low.shape[0]):
        block = jnp.concatenate([below[row], low[row], high[row], above[row]], axis=0)
        moved = dot(block, shift[...]).astype(BF16)
        for tall in range(2):
            for deep in range(4):
                at = deep * 128 + tall * 64
                to = deep * 32
                both = 2 * row + tall
                parts[both, to : to + 32, :] = moved[at + 32 : at + 64, :BREADTH]
                parts[both, 128 + to : 160 + to, :] = block[at : at + 32]
                parts[both, 256 + to : 288 + to, :] = block[at + 32 : at + 64]
                parts[both, 384 + to : 416 + to, :] = moved[at : at + 32, BREADTH:]
    for row in range(0, out.shape[0], 2):
        cells = [parts[2 * at + 1 : 2 * at + 5].reshape(2048, BREADTH) for at in (row, row + 1)]
        cells = dot(weight[...], jnp.concatenate(cells, axis=1)).astype(BF16)
        both = [
            jnp.concatenate([cells[:64, at : at + BREADTH], cells[64:, at : at + BREADTH]], axis=1)
            for at in (0, BREADTH)
        ]
        joined = dot(jnp.concatenate(both, axis=0), join[...]).astype(BF16)
        out[row] = joined[:64]
        out[row + 1] = joined[64:]


def spread_out(scale_two, scale_three, lines, two, three):
    for block in range(4):
        pair, off = divmod(block, 2)
        rows = [lines[at, 7 + pair].astype(F32)[off : off + 1] for at in range(32)]
        flat = jnp.transpose(jnp.concatenate(rows * 4, axis=0) * scale_two)
        for tap in range(27):
            a, b, e = tap // 9, (tap // 3) % 3, tap % 3
            where, slot = slot_of(b, e, a)
            if where == block:
                two[tap] = flat[slot * 16 : slot * 16 + 16, :32]
    pairs = [lines[at * 8 + group_index(), pair] for at in range(4) for pair in range(7)]
    for part in range(7):
        block = [pair.astype(F32) for pair in pairs[part * 4 : part * 4 + 4]]
        block = jnp.concatenate(block, axis=0) * scale_three
        for at in range(4):
            tap = part * 4 + at
            if tap < 27:
                b, e, a = tap // 9, (tap // 3) % 3, tap % 3
                three[a * 9 + b * 3 + e] = block[:, at * 32 : at * 32 + 32]


def shifted(axis, step):
    count = axis_count(axis)
    return [(i, i + step) for i in range(count) if 0 <= i + step < count]


def neighbours(first, last, axis):
    return (
        lax.ppermute(last, axis, shifted(axis, 1)),
        lax.ppermute(first, axis, shifted(axis, -1)),
    )


def paired(near, far, names=DEPTH):
    count = axis_count(names)
    across = [(i, i + 1) for i in range(1, count - 1, 2)]
    across += [(i + 1, i) for i in range(1, count - 1, 2)]
    return (
        lax.ppermute(near, names, [(i, i ^ 1) for i in range(count)]),
        lax.ppermute(far, names, across),
    )


def exchange(blocks, axis):
    return lax.all_to_all(blocks, axis, 0, 0, tiled=True)


def total_of(blocks):
    return jnp.sum(blocks.astype(F32), axis=0).astype(BF16)


def copied(block, names):
    return jnp.broadcast_to(block[None], (axis_count(names),) + block.shape)


def on_device(inputs, weight_two, weight_three, cotangent):
    groups = axis_count(GROUP)
    slabs = axis_count(DEPTH)
    chans, planes, height, breadth = inputs.shape
    cells = planes * slabs * height * groups * breadth
    pool_rows = height // 2
    share = weight_three.shape[3]
    filters = share * groups

    own = jnp.transpose(inputs, (2, 1, 0, 3))
    own, cotangent = lax.optimization_barrier((own, cotangent))
    rows = jax.ShapeDtypeStruct((7, planes, chans, breadth), BF16)
    near_rows, far_rows = paired(*call(sides, [rows, rows], [], (own,), 1024), GROUP)

    (packed,) = call(
        pack,
        [jax.ShapeDtypeStruct((groups, share, (pool_rows + 4) * BREADTH + 896), BF16)],
        [
            pltpu.VMEM((27, share, 32), BF16),
            pltpu.VMEM((share, pool_rows * groups, BREADTH), BF16),
            pltpu.SemaphoreType.DMA((2,)),
        ],
        (weight_three.reshape(27, share, 32), cotangent[:, 0]),
        2 * 64 * 1024,
        outside=2,
        room=56,
    )
    packed, near_rows = lax.optimization_barrier((packed, near_rows))
    arrived = exchange(packed, GROUP).reshape(filters, -1)

    plane = jax.ShapeDtypeStruct((height + 14, chans, breadth), BF16)
    near, far = paired(*call(edges, [plane, plane], [], (own, near_rows, far_rows), 1024 * 1024))

    turned = jnp.transpose(weight_two.reshape(27, 32, 16), (0, 2, 1))
    (ahead,) = call(
        weights_ahead,
        [jax.ShapeDtypeStruct((256, 1024), BF16)],
        [],
        (turned,),
        2 * 256 * 1024 * 128,
    )
    ahead, arrived = lax.optimization_barrier((ahead, arrived))

    pooled, slope, parts_two = call(
        forward_two,
        [
            jax.ShapeDtypeStruct((pool_rows + 6, 32, BREADTH), BF16),
            jax.ShapeDtypeStruct((pool_rows + 2, 256, BREADTH), F32),
            jax.ShapeDtypeStruct((height + 14, 256, BREADTH), BF16),
        ],
        [pltpu.VMEM((2 * BREADTH, 4 * BREADTH), BF16)],
        (own, near, far, near_rows, far_rows, ahead),
        2 * 14 * 256 * 1024 * 128,
    )

    pool_near, pool_far = paired(pooled, pooled)
    shift = pltpu.VMEM((BREADTH, 2 * BREADTH), BF16)
    terms = jax.ShapeDtypeStruct((pool_rows + 2, 32, BREADTH), BF16)
    grads, parts_three, to_near, same, to_far = call(
        middle_three,
        [
            jax.ShapeDtypeStruct((pool_rows + 4, filters, BREADTH), BF16),
            jax.ShapeDtypeStruct((pool_rows + 6, 288, BREADTH), BF16),
            terms,
            jax.ShapeDtypeStruct(terms.shape, F32),
            terms,
        ],
        [
            shift,
            pltpu.VMEM((pool_rows + 4, 3 * filters, BREADTH), BF16),
            pltpu.VMEM((96, 9 * filters), BF16),
        ],
        (pool_near, pooled, pool_far, arrived),
        2 * 12 * 64 * 864 * 128 * 2,
    )

    terms_near, terms_far = paired(to_near, to_far)
    (local_three,) = call(
        filters_three,
        [jax.ShapeDtypeStruct((filters, 1024), F32)],
        [],
        (grads, parts_three),
        2 * 8 * 64 * 864 * 128,
    )
    plane = jax.ShapeDtypeStruct((pool_rows + 2, 128, BREADTH), BF16)
    low, high, lines = call(
        middle_two,
        [plane, plane, jax.ShapeDtypeStruct((32, 18, BREADTH), F32)],
        [],
        (terms_near, same, terms_far, slope, parts_two, local_three),
        2 * 8 * 256 * 1024 * 128,
    )

    two_below, two_above = neighbours(low, high, DEPTH)
    lines = lines.astype(BF16).reshape(32, 9, 2, BREADTH)
    lines = total_of(exchange(lines, NEAR))
    lines = total_of(exchange(copied(lines, ("z",)), "z"))
    lines = exchange(copied(lines, NEAR), NEAR)
    two, three = call(
        functools.partial(spread_out, 1.0 / math.sqrt(cells), 1.0 / math.sqrt(cells / 8)),
        [
            jax.ShapeDtypeStruct((27, 16, 32), F32),
            jax.ShapeDtypeStruct((27, share, 32), F32),
        ],
        [],
        (lines,),
        2 * 64 * 1024,
    )

    (cells_back,) = call(
        backward_two,
        [jax.ShapeDtypeStruct((pool_rows, 64, 2 * BREADTH), BF16)],
        [
            pltpu.VMEM((height + 4, 512, BREADTH), BF16),
            shift,
            pltpu.VMEM((2 * BREADTH, 2 * BREADTH), BF16),
            pltpu.VMEM((128, 2048), BF16),
        ],
        (two_below, low, high, two_above, turned),
        2 * 8 * 128 * 2048 * 128,
    )
    input_grad = jnp.transpose(
        cells_back.reshape(pool_rows, 2, 2, chans, breadth), (3, 1, 0, 2, 4)
    ).reshape(inputs.shape)
    weight_grad_two = jnp.transpose(two, (0, 2, 1)).reshape(weight_two.shape)
    return (input_grad, weight_grad_two, three.reshape(weight_three.shape))


def solution(mesh):
    parts = jax.sharding.Mesh(mesh.devices.reshape(2, 16, 2, 2, 4), DEPTH + GROUP)
    placed = (
        P(None, DEPTH, GROUP, None),
        P(),
        P(None, None, None, GROUP, None),
        P(GROUP, DEPTH, None, None),
    )
    return jax.shard_map(
        on_device,
        mesh=parts,
        in_specs=placed,
        out_specs=(P(None, DEPTH, GROUP, None), P(), P(None, None, None, GROUP, None)),
        check_vma=False,
    )
```

```python
import functools
import math

import jax
import jax.numpy as jnp
from jax import lax
from jax.experimental import pallas as pl
from jax.experimental.pallas import tpu as pltpu
from jax.sharding import PartitionSpec as P


F32 = jnp.float32
BF16 = jnp.bfloat16
BREADTH = 128
DEPTH = ("yl", "z", "core")
GROUP = ("yh", "x")
NEAR = ("yl", "core", "yh", "x")


def axis_count(names):
    return math.prod(lax.axis_size(name) for name in names)


def group_index():
    return lax.axis_index("yh") * lax.axis_size("x") + lax.axis_index("x")


def call(kernel, outs, scratch, args, flops, outside=0, room=16):
    specs = [pl.BlockSpec(memory_space=pl.ANY)] * outside
    specs += [pl.BlockSpec(memory_space=pltpu.VMEM)] * (len(args) - outside)
    moved = sum(math.prod(a.shape) * a.dtype.itemsize for a in list(args) + list(outs))
    return pl.pallas_call(
        kernel,
        out_shape=outs,
        in_specs=specs,
        out_specs=[pl.BlockSpec(memory_space=pltpu.VMEM)] * len(outs),
        scratch_shapes=scratch,
        compiler_params=pltpu.CompilerParams(vmem_limit_bytes=room * 1024 * 1024),
        cost_estimate=pl.CostEstimate(flops=flops, bytes_accessed=moved, transcendentals=0),
    )(*args)


def dot(left, right):
    return jnp.dot(left, right, preferred_element_type=F32)


def dot_nt(left, right):
    return lax.dot_general(left, right, (((1,), (1,)), ((), ())), preferred_element_type=F32)


def dot_tn(left, right):
    return lax.dot_general(left, right, (((0,), (0,)), ((), ())), preferred_element_type=F32)


def indicator(shape, test):
    row = lax.broadcasted_iota(jnp.int32, shape, 0)
    col = lax.broadcasted_iota(jnp.int32, shape, 1)
    return jnp.where(test(row, col), 1.0, 0.0).astype(BF16)


def splitter():
    def test(row, col):
        part, at = col // BREADTH, col % BREADTH
        return row == 2 * at + part - 1

    return indicator((2 * BREADTH, 4 * BREADTH), test)


def shifter():
    def test(row, col):
        part, at = col // BREADTH, col % BREADTH
        return row == at + 2 * part - 1

    return indicator((BREADTH, 2 * BREADTH), test)


def joiner():
    def test(row, col):
        return col == 2 * (row % BREADTH) + row // BREADTH

    return indicator((2 * BREADTH, 2 * BREADTH), test)


def weights_two(out, turned, flip):
    outs, ins = (16, 32) if flip else (32, 16)
    per = BREADTH // ins
    total = []
    for part in range(64 // per):
        summed = jnp.zeros((outs, BREADTH), F32)
        for at in range(per):
            place = part * per + at
            b, e, a = place // 16, (place // 4) % 4, place % 4
            if max(a, b, e) > 2:
                continue
            if flip:
                a, b, e = 2 - a, 2 - b, 2 - e
            spread = indicator((ins, BREADTH), lambda row, col: col == row + at * ins)
            tap = turned[a * 9 + b * 3 + e]
            summed = summed + (dot(tap, spread) if flip else dot_tn(tap, spread))
        total.append(summed)
    base = jnp.concatenate(total, axis=1)
    for phase in range(8):
        deep, high, wide = phase // 4, (phase // 2) % 2, phase % 2
        move = (high * 16 + wide * 4 + deep) * ins
        full = pltpu.roll(base, move, 1) if move else base
        at = (wide * 4 + deep * 2 + high if flip else phase) * outs
        out[at : at + outs, :] = full.astype(BF16)


def weights_ahead(turned, out):
    weights_two(out, turned, False)


def inside(at, rows):
    return jnp.logical_and(at >= 0, at < rows * axis_count(GROUP))


def sides(own, near, far):
    odd = lax.rem(lax.axis_index("x"), 2)
    rest = own.shape[0] - near.shape[0]
    for row in range(near.shape[0]):
        near[row] = own[row + rest * (1 - odd)]
        far[row] = own[row + rest * odd]


def edges(own, near_rows, far_rows, far, near):
    core = lax.axis_index("core")
    top, bottom = in_order(near_rows, far_rows, "x")
    count, height = near_rows.shape[0], own.shape[0]
    for row in range(count):
        near[row] = top(row, 1 - core)
        far[row] = top(row, core)
        near[count + height + row] = bottom(row, 1 - core)
        far[count + height + row] = bottom(row, core)
    for row in range(height):
        near[count + row] = own[row, 1 - core]
        far[count + row] = own[row, core]


def in_order(near, far, name="core"):
    lower = lax.rem(lax.axis_index(name), 2) == 0

    def below(*at):
        return lax.select(lower, far[at], near[at])

    def above(*at):
        return lax.select(lower, near[at], far[at])

    return below, above


def forward_two(own, far, near, near_rows, far_rows, weight, pooled, slope, parts, split):
    split[...] = splitter()
    first = pooled.shape[0] - 6
    first = first * group_index() - 3
    edge = near_rows.shape[0]
    height = own.shape[0]
    below, above = in_order(near, far)
    top, bottom = in_order(near_rows, far_rows, "x")

    def place(row, many, block):
        cells = dot(block, split[...]).astype(BF16).reshape(many, 64, 4 * BREADTH)
        for part in range(4):
            to = part * 64
            parts[row : row + many, to : to + 64, :] = cells[:, :, part * BREADTH : (part + 1) * BREADTH]

    for taken, to, many in ((top, 0, edge), (own, edge, height), (bottom, edge + height, edge)):
        for row in range(0, many, 4):
            block = []
            for at in range(row, min(row + 4, many)):
                if taken is own:
                    both = [own[at, 0], own[at, 1]]
                else:
                    both = [taken(at, 0), taken(at, 1)]
                block += [below(to + at)] + both + [above(to + at)]
            place(to + row, len(block) // 4, jnp.concatenate(block, axis=0))

    rows = pooled.shape[0]
    for row in range(0, rows, 2):
        cells = [parts[2 * at : 2 * at + 4].reshape(1024, BREADTH) for at in (row, row + 1)]
        pre = dot(weight[...], jnp.concatenate(cells, axis=1))
        small = jnp.exp(-jnp.abs(pre))
        whole = 1.0 + small
        value = 0.3 * pre + 0.7 * (jnp.maximum(pre, 0.0) + jnp.log(whole))
        summed = jnp.sum(value.reshape(8, 32, 2 * BREADTH), axis=0) * 0.125
        for off in range(2):
            half = summed[:, off * BREADTH : (off + 1) * BREADTH]
            kept = inside(first + row + off, rows - 6)
            pooled[row + off] = jnp.where(kept, half, 0.0).astype(BF16)
        if 2 <= row < rows - 2:
            rate = 0.3 + 0.7 * (jnp.where(pre >= 0.0, 1.0, small) / whole)
            slope[row - 2] = rate[:, :BREADTH]
            slope[row - 1] = rate[:, BREADTH:]


def place_shifted(planes, rows, parts, shift, chans):
    span = len(planes) * chans
    step = 256 // chans
    for plane, taken in enumerate(planes):
        at = plane * chans
        for row in range(0, rows, step):
            many = min(step, rows - row)
            block = taken(slice(row, row + many))
            moved = dot(block.reshape(many * chans, BREADTH), shift[...]).astype(BF16)
            moved = moved.reshape(many, chans, 2 * BREADTH)
            parts[row : row + many, at : at + chans, :] = moved[:, :, :BREADTH]
            parts[row : row + many, span + at : span + at + chans, :] = block
            parts[row : row + many, 2 * span + at : 2 * span + at + chans, :] = moved[:, :, BREADTH:]


def side_by_side(parts, row, many, taken, step=1):
    size = taken * parts.shape[1]
    return jnp.concatenate(
        [parts[at * step : at * step + taken].reshape(size, BREADTH) for at in range(row, row + many)],
        axis=1,
    )


def pack(taps_in, cot_in, out, taps, rows_in, done):
    copies = [
        pltpu.make_async_copy(cot_in, rows_in, done.at[0]),
        pltpu.make_async_copy(taps_in, taps, done.at[1]),
    ]
    for copy in copies:
        copy.start()
    copies[0].wait()
    count, share, width = out.shape
    cot = jnp.swapaxes(rows_in[...].astype(F32), 0, 1).astype(BF16)
    rows = cot.shape[0] // count
    extra = (width - 896) // BREADTH - rows
    for to in range(count):
        for row in range(rows + extra):
            at = rows * to - extra // 2 + row
            lane = row * BREADTH
            if 0 <= at < cot.shape[0]:
                out[to, :, lane : lane + BREADTH] = cot[at]
            else:
                out[to, :, lane : lane + BREADTH] = jnp.zeros((share, BREADTH), BF16)
    copies[1].wait()
    blocks = []
    for part in range(7):
        piece = []
        for tap in range(part * 4, part * 4 + 4):
            at = (tap % 3) * 9 + (tap // 9) * 3 + (tap // 3) % 3
            piece.append(taps[at].astype(F32) if tap < 27 else jnp.zeros((share, 32), F32))
        blocks.append(jnp.concatenate(piece, axis=1).astype(BF16))
    for to in range(count):
        for part in range(7):
            lane = (rows + extra + part) * BREADTH
            out[to, :, lane : lane + BREADTH] = blocks[part]


def middle_three(near, own, far, arrived, grads, parts, to_far, same, to_near, shift, around, turned):
    shift[...] = shifter()
    below, above = in_order(near, far)
    place_shifted((below, own.__getitem__, above), own.shape[0], parts, shift, 32)
    rows = grads.shape[0]
    lower = lax.axis_index("core") == 0
    span = rows * BREADTH
    weight = arrived[:, span:]
    for row in range(0, rows, 4):
        pre = dot(weight[:, :864], side_by_side(parts, row, 4, 3))
        small = jnp.exp(-jnp.abs(pre))
        rate = 0.3 + 0.7 * (jnp.where(pre >= 0.0, 1.0, small) / (1.0 + small))
        full = arrived[:, row * BREADTH : (row + 4) * BREADTH].astype(F32) * rate
        for off in range(4):
            grads[row + off] = full[:, off * BREADTH : (off + 1) * BREADTH].astype(BF16)
    weight = weight.astype(F32)
    flat = jnp.transpose(jnp.concatenate([weight, weight], axis=0))
    lane = lax.broadcasted_iota(jnp.int32, (32, BREADTH), 1)
    for plane in range(3):

        def tap(at, plane=plane):
            first = ((8 - at) * 3 + 2 - plane) * 32
            return flat[first : first + 32]

        to = plane * 32
        for at in range(0, 8, 2):
            pair = jnp.where(lane < 64, tap(at), tap(at + 1))
            turned[to : to + 32, at * 64 : at * 64 + 128] = pair.astype(BF16)
        turned[to : to + 32, 512:576] = tap(8)[:, :64].astype(BF16)
    place_shifted((grads.__getitem__,), rows, around, shift, 64)
    for row in range(0, rows - 2, 2):
        pool = dot(turned[...], side_by_side(around, row, 2, 3))
        for off in range(2):
            half = pool[:, off * BREADTH : (off + 1) * BREADTH]
            up, down = half[:32], half[64:]
            same[row + off] = half[32:64]
            to_near[row + off] = lax.select(lower, up, down).astype(BF16)
            to_far[row + off] = lax.select(lower, down, up).astype(BF16)


def filters_three(grads, parts, out):
    rows = grads.shape[0]
    left = jnp.concatenate([grads[row] for row in range(2, rows - 2)], axis=1)
    full = dot_nt(left, side_by_side(parts, 2, rows - 4, 3))
    out[:, :864] = full
    out[:, 864:] = jnp.zeros((full.shape[0], 160), F32)


def middle_two(near, own, far, slope, parts, three, low, high, lines):
    rows = own.shape[0] - 2
    first = rows * group_index() - 1
    left = []
    for row in range(rows + 2):
        pool = own[row] + near[row].astype(F32) + far[row].astype(F32)
        pool = jnp.where(inside(first + row, rows), pool, 0.0) * 0.125
        full = pool[None] * slope[row].reshape(8, 32, BREADTH)
        full = full.astype(BF16).reshape(256, BREADTH)
        low[row] = full[:128]
        high[row] = full[128:]
        if 1 <= row <= rows:
            left.append(full)
    left = jnp.concatenate(left, axis=1)
    blocks = []
    for off in range(4):
        right = jnp.concatenate([parts[2 * row + 4 + off] for row in range(1, rows + 1)], axis=1)
        blocks.append(dot_nt(left, right))
    total = jnp.zeros((32, 768), F32)
    for phase in range(8):
        deep, tall, wide = phase // 4, (phase // 2) % 2, phase % 2
        part = jnp.concatenate(
            [block[phase * 32 : phase * 32 + 32] for block in blocks[tall : tall + 3]], axis=1
        )
        move = (wide * 4 + deep) * 16
        if move:
            part = pltpu.roll(part, 768 - move, 1)
        total = total + part
    slot = lax.broadcasted_iota(jnp.int32, (32, BREADTH), 1) // 16
    dense = []
    rest = jnp.zeros((32, BREADTH), F32)
    for off in range(3):
        one = total[:, off * 256 : off * 256 + 128]
        two = total[:, off * 256 + 128 : off * 256 + 256]
        one = jnp.where(slot == 3, pltpu.roll(two, 48, 1), one)
        dense.append(jnp.where(slot == 7, pltpu.roll(two, 96, 1), one))
        moved = pltpu.roll(two, 96 + off * 16, 1) if off != 2 else two
        rest = jnp.where(slot == off, moved, rest)
    dense.append(rest)
    for to in range(32):
        quarter, group = to // 8, to % 8
        row = 0
        while row < 14:
            part, off = divmod(quarter * 14 + row, 8)
            many = min(8 - off, 14 - row)
            at, lane = group * 8 + off, part * BREADTH
            lines[to, row : row + many, :] = three[at : at + many, lane : lane + BREADTH]
            row += many
        for block in range(4):
            lines[to, 14 + block : 15 + block, :] = dense[block][to : to + 1]


def slot_of(b, e, a):
    if e < 2:
        return b, e * 4 + a
    return ((b, 3), (b, 7), (3, b))[a]


def backward_two(below, low, high, above, turned, out, parts, shift, join, weight):
    weights_two(weight, turned, True)
    shift[...] = shifter()
    join[...] = joiner()
    for row in range(low.shape[0]):
        block = jnp.concatenate([below[row], low[row], high[row], above[row]], axis=0)
        moved = dot(block, shift[...]).astype(BF16)
        for tall in range(2):
            for deep in range(4):
                at = deep * 128 + tall * 64
                to = deep * 32
                both = 2 * row + tall
                parts[both, to : to + 32, :] = moved[at + 32 : at + 64, :BREADTH]
                parts[both, 128 + to : 160 + to, :] = block[at : at + 32]
                parts[both, 256 + to : 288 + to, :] = block[at + 32 : at + 64]
                parts[both, 384 + to : 416 + to, :] = moved[at : at + 32, BREADTH:]
    for row in range(0, out.shape[0], 2):
        cells = [parts[2 * at + 1 : 2 * at + 5].reshape(2048, BREADTH) for at in (row, row + 1)]
        cells = dot(weight[...], jnp.concatenate(cells, axis=1)).astype(BF16)
        both = [
            jnp.concatenate([cells[:64, at : at + BREADTH], cells[64:, at : at + BREADTH]], axis=1)
            for at in (0, BREADTH)
        ]
        joined = dot(jnp.concatenate(both, axis=0), join[...]).astype(BF16)
        out[row] = joined[:64]
        out[row + 1] = joined[64:]


def spread_out(scale_two, scale_three, lines, two, three):
    for block in range(4):
        pair, off = divmod(block, 2)
        rows = [lines[at, 7 + pair].astype(F32)[off : off + 1] for at in range(32)]
        flat = jnp.transpose(jnp.concatenate(rows * 4, axis=0) * scale_two)
        for tap in range(27):
            a, b, e = tap // 9, (tap // 3) % 3, tap % 3
            where, slot = slot_of(b, e, a)
            if where == block:
                two[tap] = flat[slot * 16 : slot * 16 + 16, :32]
    pairs = [lines[at * 8 + group_index(), pair] for at in range(4) for pair in range(7)]
    for part in range(7):
        block = [pair.astype(F32) for pair in pairs[part * 4 : part * 4 + 4]]
        block = jnp.concatenate(block, axis=0) * scale_three
        for at in range(4):
            tap = part * 4 + at
            if tap < 27:
                b, e, a = tap // 9, (tap // 3) % 3, tap % 3
                three[a * 9 + b * 3 + e] = block[:, at * 32 : at * 32 + 32]


def shifted(axis, step):
    count = axis_count(axis)
    return [(i, i + step) for i in range(count) if 0 <= i + step < count]


def neighbours(first, last, axis):
    return (
        lax.ppermute(last, axis, shifted(axis, 1)),
        lax.ppermute(first, axis, shifted(axis, -1)),
    )


def paired(near, far, names=DEPTH):
    count = axis_count(names)
    across = [(i, i + 1) for i in range(1, count - 1, 2)]
    across += [(i + 1, i) for i in range(1, count - 1, 2)]
    far = lax.ppermute(far, names, across)
    near = lax.ppermute(near, names, [(i, i ^ 1) for i in range(count)])
    return near, far


def exchange(blocks, axis):
    return lax.all_to_all(blocks, axis, 0, 0, tiled=True)


def total_of(blocks):
    return jnp.sum(blocks.astype(F32), axis=0).astype(BF16)


def copied(block, names):
    return jnp.broadcast_to(block[None], (axis_count(names),) + block.shape)


def on_device(inputs, weight_two, weight_three, cotangent):
    groups = axis_count(GROUP)
    slabs = axis_count(DEPTH)
    chans, planes, height, breadth = inputs.shape
    cells = planes * slabs * height * groups * breadth
    pool_rows = height // 2
    share = weight_three.shape[3]
    filters = share * groups

    own = jnp.transpose(inputs, (2, 1, 0, 3))
    own, cotangent = lax.optimization_barrier((own, cotangent))
    rows = jax.ShapeDtypeStruct((7, planes, chans, breadth), BF16)
    near_rows, far_rows = paired(*call(sides, [rows, rows], [], (own,), 1024), GROUP)

    (packed,) = call(
        pack,
        [jax.ShapeDtypeStruct((groups, share, (pool_rows + 4) * BREADTH + 896), BF16)],
        [
            pltpu.VMEM((27, share, 32), BF16),
            pltpu.VMEM((share, pool_rows * groups, BREADTH), BF16),
            pltpu.SemaphoreType.DMA((2,)),
        ],
        (weight_three.reshape(27, share, 32), cotangent[:, 0]),
        2 * 64 * 1024,
        outside=2,
        room=56,
    )
    packed, near_rows = lax.optimization_barrier((packed, near_rows))
    arrived = exchange(packed, GROUP).reshape(filters, -1)

    plane = jax.ShapeDtypeStruct((height + 14, chans, breadth), BF16)
    far, near = call(edges, [plane, plane], [], (own, near_rows, far_rows), 1024 * 1024)
    near, far = paired(near, far)

    turned = jnp.transpose(weight_two.reshape(27, 32, 16), (0, 2, 1))
    (ahead,) = call(
        weights_ahead,
        [jax.ShapeDtypeStruct((256, 1024), BF16)],
        [],
        (turned,),
        2 * 256 * 1024 * 128,
    )
    ahead, arrived = lax.optimization_barrier((ahead, arrived))

    pooled, slope, parts_two = call(
        forward_two,
        [
            jax.ShapeDtypeStruct((pool_rows + 6, 32, BREADTH), BF16),
            jax.ShapeDtypeStruct((pool_rows + 2, 256, BREADTH), F32),
            jax.ShapeDtypeStruct((height + 14, 256, BREADTH), BF16),
        ],
        [pltpu.VMEM((2 * BREADTH, 4 * BREADTH), BF16)],
        (own, far, near, near_rows, far_rows, ahead),
        2 * 14 * 256 * 1024 * 128,
    )

    pool_near, pool_far = paired(pooled, pooled)
    shift = pltpu.VMEM((BREADTH, 2 * BREADTH), BF16)
    terms = jax.ShapeDtypeStruct((pool_rows + 2, 32, BREADTH), BF16)
    grads, parts_three, to_far, same, to_near = call(
        middle_three,
        [
            jax.ShapeDtypeStruct((pool_rows + 4, filters, BREADTH), BF16),
            jax.ShapeDtypeStruct((pool_rows + 6, 288, BREADTH), BF16),
            terms,
            jax.ShapeDtypeStruct(terms.shape, F32),
            terms,
        ],
        [
            shift,
            pltpu.VMEM((pool_rows + 4, 3 * filters, BREADTH), BF16),
            pltpu.VMEM((96, 9 * filters), BF16),
        ],
        (pool_near, pooled, pool_far, arrived),
        2 * 12 * 64 * 864 * 128 * 2,
    )

    terms_near, terms_far = paired(to_near, to_far)
    (local_three,) = call(
        filters_three,
        [jax.ShapeDtypeStruct((filters, 1024), F32)],
        [],
        (grads, parts_three),
        2 * 8 * 64 * 864 * 128,
    )
    plane = jax.ShapeDtypeStruct((pool_rows + 2, 128, BREADTH), BF16)
    low, high, lines = call(
        middle_two,
        [plane, plane, jax.ShapeDtypeStruct((32, 18, BREADTH), F32)],
        [],
        (terms_far, same, terms_near, slope, parts_two, local_three),
        2 * 8 * 256 * 1024 * 128,
    )

    two_below, two_above = neighbours(low, high, DEPTH)
    lines = lines.astype(BF16).reshape(32, 9, 2, BREADTH)
    lines = total_of(exchange(lines, NEAR))
    lines = total_of(exchange(copied(lines, ("z",)), "z"))
    lines = exchange(copied(lines, NEAR), NEAR)
    two, three = call(
        functools.partial(spread_out, 1.0 / math.sqrt(cells), 1.0 / math.sqrt(cells / 8)),
        [
            jax.ShapeDtypeStruct((27, 16, 32), F32),
            jax.ShapeDtypeStruct((27, share, 32), F32),
        ],
        [],
        (lines,),
        2 * 64 * 1024,
    )

    (cells_back,) = call(
        backward_two,
        [jax.ShapeDtypeStruct((pool_rows, 64, 2 * BREADTH), BF16)],
        [
            pltpu.VMEM((height + 4, 512, BREADTH), BF16),
            shift,
            pltpu.VMEM((2 * BREADTH, 2 * BREADTH), BF16),
            pltpu.VMEM((128, 2048), BF16),
        ],
        (two_below, low, high, two_above, turned),
        2 * 8 * 128 * 2048 * 128,
    )
    input_grad = jnp.transpose(
        cells_back.reshape(pool_rows, 2, 2, chans, breadth), (3, 1, 0, 2, 4)
    ).reshape(inputs.shape)
    weight_grad_two = jnp.transpose(two, (0, 2, 1)).reshape(weight_two.shape)
    return (input_grad, weight_grad_two, three.reshape(weight_three.shape))


def solution(mesh):
    parts = jax.sharding.Mesh(mesh.devices.reshape(2, 16, 2, 2, 4), DEPTH + GROUP)
    placed = (
        P(None, DEPTH, GROUP, None),
        P(),
        P(None, None, None, GROUP, None),
        P(GROUP, DEPTH, None, None),
    )
    return jax.shard_map(
        on_device,
        mesh=parts,
        in_specs=placed,
        out_specs=(P(None, DEPTH, GROUP, None), P(), P(None, None, None, GROUP, None)),
        check_vma=False,
    )
```
